256 devices in a mesh: pts: 256 (over z, y, x, core).
Axes of the slice: x: 4, y: 4, z: 8, core: 2. Of those that a mesh axis runs over, the one named last changes fastest.
Arguments:
- embeddings: bfloat16 [262144, 384], P('pts'), may hold values from -1 to 1, as said below
- site_ids: int32 [262144], P('pts'), may hold values from 0 to 63
- inv_scale: float32 [384], replicated, may hold values from 0.5 to 2
- noise: float32 [128], replicated, may hold values from 0.5 to 2
- solution: float32 [262144, 128], P('pts'), may hold values from -6 to 6
- residual: float32 [262144, 128], P('pts'), may hold values from -9 to 9, as said below
- direction: float32 [262144, 128], P('pts'), may hold values from -9 to 9, as said below
Outputs:
- new_solution: float32 [262144, 128], P('pts')
- new_residual: float32 [262144, 128], P('pts')
- new_direction: float32 [262144, 128], P('pts')
- new_norms: float32 [128], replicated
The draws below stay inside these ranges and needn't reach their ends.
Inputs may be any that keep to these rules, and one draw needn't show every extreme that they name: `embeddings`: real values. `residual`: real values. Entries drawn independently of the embeddings; in every column the sum of direction times applied is positive.
All inputs are finite; a program needn't handle non-finite values.
Results may differ from the reference program's by a relative error of at most 0.0085.
Values may be sent and summed in bfloat16 or wider, within the bound.
A program may use at most 64 MiB of HBM per device.

```python
import math
import jax
import jax.numpy as jnp
from jax import lax

F = 384
R = 128
P_DEV = 1024
SITES = 64
POINTS = 262144
N_PTS = 256


def rising_rows():
    position = jnp.arange(POINTS, dtype=jnp.float32) / POINTS
    return 0.6 + 0.8 * position


def draw_normal_rows(key):
    values = jnp.clip(jax.random.normal(key, (POINTS, R), jnp.float32), -6.0, 6.0)
    return values * rising_rows()[:, None]


def draw_embeddings(key, part):
    key = jax.random.fold_in(key, 5)
    member_key, centre_key, gain_key, spread_key, jitter_key = jax.random.split(key, 5)
    groups = max(P_DEV // 4, 2)
    member = jax.random.randint(member_key, (POINTS,), 0, groups)
    centre_scale = 1.8 / math.sqrt(F)
    jitter_scale = 0.18 / math.sqrt(F)
    centres = jnp.clip(jax.random.normal(centre_key, (groups, F), jnp.float32), -3.0, 3.0)
    gains = jnp.exp(jax.random.uniform(gain_key, (groups,), jnp.float32, math.log(0.7), math.log(1.4)))
    spreads = jnp.exp(jax.random.uniform(spread_key, (POINTS,), jnp.float32, math.log(0.5), math.log(2.0)))
    jitter = jnp.clip(jax.random.normal(jitter_key, (POINTS, F), jnp.float32), -3.0, 3.0)
    placed = centres * (centre_scale * gains)[:, None]
    rows = jnp.take(placed, member, axis=0) + jitter * (jitter_scale * spreads)[:, None]
    return jnp.clip(rows, -1.0, 1.0).astype(jnp.bfloat16)


def draw_residual(key, part):
    key = jax.random.fold_in(key, 11)
    return draw_normal_rows(key).astype(jnp.float32)


def draw_direction(key, part):
    key = jax.random.fold_in(key, 23)
    return draw_normal_rows(key).astype(jnp.float32)


def touch_ends(values, own_key, smallest, top_value):
    spot = [jax.random.randint(jax.random.fold_in(own_key, axis), (), 0, length) for axis, length in enumerate(values.shape)]
    longest = values.shape.index(max(values.shape))
    beside = spot[:longest] + [(spot[longest] + 1) % values.shape[longest]] + spot[longest + 1:]
    return values.at[tuple(spot)].set(smallest).at[tuple(beside)].set(top_value)


def block_levels(key, extent, shards, low, high):
    loudness = 1.0
    for dim, parts in shards:
        draws = jax.random.uniform(jax.random.fold_in(jax.random.fold_in(key, 6), dim), (parts,), jnp.float32, low / len(shards), high / len(shards))
        loudness = loudness * jnp.repeat(jnp.exp(draws), extent[dim] // parts).reshape((-1,) + (1,) * (len(extent) - 1 - dim))
    return loudness


def bell_draw(own_key, extent, scale, bound, cuts=(), held_as=jnp.bfloat16):
    entries = scale * jax.random.normal(own_key, extent, jnp.float32)
    if cuts:
        entries = entries * block_levels(own_key, extent, cuts, -0.22, 0.18)
    return jnp.clip(entries, -bound, bound).astype(held_as)


def setup_inputs(seed: int = 0) -> dict:
    seeds = jax.random.split(jax.random.key(seed), 8)
    embeddings = draw_embeddings(jax.random.fold_in(seeds[7], 71), 0)
    site_ids = touch_ends(jax.random.randint(seeds[1], (POINTS,), 0, SITES), jax.random.fold_in(seeds[1], 1), 0, SITES - 1).astype(jnp.int32)
    inv_scale = jnp.clip(jnp.exp(jax.random.uniform(seeds[2], (F,), jnp.float32, math.log(0.5), math.log(2.0))), 0.5, 2.0)
    noise = jnp.clip(jnp.exp(jax.random.uniform(seeds[3], (R,), jnp.float32, math.log(0.5), math.log(2.0))), 0.5, 2.0)
    solution = bell_draw(seeds[4], (POINTS, R), 1.0, 6.0, ((0, 256),), jnp.float32)
    residual = draw_residual(jax.random.fold_in(seeds[7], 71), 0)
    direction = draw_direction(jax.random.fold_in(seeds[7], 71), 0)
    return dict(embeddings=embeddings, site_ids=site_ids, inv_scale=inv_scale, noise=noise, solution=solution, residual=residual, direction=direction)


root_three = math.sqrt(3.0)
site_weight = 0.5

def kernel_tile(left_rows, left_norms, left_sites, right_rows, right_norms, right_sites):
    cross = jnp.dot(left_rows, right_rows.T, preferred_element_type=jnp.float32)
    squared = jnp.maximum(left_norms[:, None] + right_norms[None, :] - 2.0 * cross, 0.0)
    distance = jnp.sqrt(squared)
    matern = (1.0 + root_three * distance) * jnp.exp(-root_three * distance)
    same_site = (left_sites[:, None] == right_sites[None, :]).astype(jnp.float32)
    return (matern + site_weight * same_site).astype(jnp.bfloat16)

def reference(embeddings, site_ids, inv_scale, noise, solution, residual, direction):
    scaled = (embeddings.astype(jnp.float32) * inv_scale).astype(jnp.bfloat16)
    sq_norms = lax.optimization_barrier(jnp.sum(jnp.square(scaled.astype(jnp.float32)), axis=1))
    dir_low = direction.astype(jnp.bfloat16)
    feature_blocks = scaled.reshape(N_PTS, P_DEV, F)
    norm_blocks = sq_norms.reshape(N_PTS, P_DEV)
    site_blocks = site_ids.reshape(N_PTS, P_DEV)
    dir_blocks = dir_low.reshape(N_PTS, P_DEV, R)

    def nearby_terms(block_index):
        below = (block_index - 1) % N_PTS
        self_tile = kernel_tile(feature_blocks[block_index], norm_blocks[block_index], site_blocks[block_index], feature_blocks[block_index], norm_blocks[block_index], site_blocks[block_index])
        lower_tile = kernel_tile(feature_blocks[block_index], norm_blocks[block_index], site_blocks[block_index], feature_blocks[below], norm_blocks[below], site_blocks[below])
        local_terms = jnp.dot(self_tile, dir_blocks[block_index], preferred_element_type=jnp.float32)
        local_terms = local_terms + jnp.dot(lower_tile, dir_blocks[below], preferred_element_type=jnp.float32)
        back_terms = jnp.dot(lower_tile.T, dir_blocks[block_index], preferred_element_type=jnp.float32)
        return (local_terms, back_terms)
    local_terms, back_terms = lax.map(nearby_terms, jnp.arange(N_PTS, dtype=jnp.int32))
    midway = N_PTS // 2

    def opposite_terms(block_index):
        other = block_index + midway
        pair_tile = kernel_tile(feature_blocks[block_index], norm_blocks[block_index], site_blocks[block_index], feature_blocks[other], norm_blocks[other], site_blocks[other])
        first = jnp.dot(pair_tile, dir_blocks[other], preferred_element_type=jnp.float32)
        second = jnp.dot(pair_tile.T, dir_blocks[block_index], preferred_element_type=jnp.float32)
        return (first, second)
    first_half, second_half = lax.map(opposite_terms, jnp.arange(midway, dtype=jnp.int32))
    far_terms = jnp.concatenate([first_half, second_half], axis=0)
    products = local_terms + jnp.roll(back_terms, -1, axis=0) + far_terms
    applied = noise * direction + products.reshape(POINTS, R)
    old_norms = lax.optimization_barrier(jnp.sum(residual * residual, axis=0))
    curvature = lax.optimization_barrier(jnp.sum(direction * applied, axis=0))
    step_size = old_norms / curvature
    new_solution = solution + step_size * direction
    new_residual = residual - step_size * applied
    new_norms = lax.optimization_barrier(jnp.sum(new_residual * new_residual, axis=0))
    new_direction = new_residual + new_norms / old_norms * direction
    return (new_solution, new_residual, new_direction, new_norms)
```

```python
import functools
import math

import jax
import jax.numpy as jnp
from jax import lax
from jax.experimental import pallas as pl
from jax.experimental.pallas import tpu as pltpu
from jax.sharding import PartitionSpec as P

root_three = math.sqrt(3.0)
site_weight = 0.5
sites = 64

MESH = pl.DeviceIdType.MESH
ZS, YS, XS, CS = 8, 4, 4, 2
PLANE = YS * XS * CS
PTS = ZS * PLANE
ROWS = 1024
F = 384
R = 128
CHUNK = 256
CHUNKS = ROWS // CHUNK
f32 = jnp.float32
bf16 = jnp.bfloat16


def dot(a, b):
    return jnp.dot(a, b, preferred_element_type=f32)


def matern(left, right, left_norms, right_norms):
    cross = lax.dot_general(left, right, (((1,), (1,)), ((), ())), preferred_element_type=f32)
    squared = jnp.maximum(cross + left_norms + right_norms, 1e-30)
    distance = squared * lax.rsqrt(squared)
    decay = jnp.exp2(distance * (-root_three * math.log2(math.e)))
    return ((1.0 + root_three * distance) * decay).astype(bf16)


def one_hot(ids):
    rows = lax.broadcasted_iota(jnp.int32, (2 * sites, ids.shape[1]), 0) % sites
    return (rows.astype(f32) == ids).astype(bf16)


def split_halves(totals):
    high = totals.astype(bf16)
    low = (totals - high.astype(f32)).astype(bf16)
    rows = lax.broadcasted_iota(jnp.int32, totals.shape, 0)
    return jnp.where(rows < sites, high, low)


def kernel(
    emb_hbm, dir_hbm, res_hbm, ids_ref, scale_ref, noise_ref,
    applied_ref, sums_ref,
    emb, direction, residual, own, left, norm_col, dir_t, own_meta,
    near, near_meta, far, far_meta, ret_out, ret_in, acc, totals, first, second,
    load_sem, near_send, near_recv, near_meta_send, near_meta_recv,
    far_send, far_recv, far_meta_send, far_meta_recv,
    ret_send, ret_recv, sum_send, sum_recv,
):
    me = lax.axis_index("pts")
    core = me % CS
    plane = me // PLANE
    spot = (me // CS) % (YS * XS)

    twin = me + 1 - 2 * core
    step = 2 * core - 1
    beside = (me + step + PTS) % PTS
    opposite = (me + PTS // 2) % PTS
    sends = (me // (PTS // 2) + me) % 2 == 0
    receives = jnp.logical_not(sends)

    column_place = plane * CS + core
    column = [
        ((plane + dz) % ZS) * PLANE + spot * CS + (core + dc) % CS
        for dz in range(ZS) for dc in range(CS) if dz or dc
    ]
    layer = [
        plane * PLANE + ((spot + k) % (YS * XS)) * CS + core for k in range(1, YS * XS)
    ]

    loads = [
        pltpu.make_async_copy(src, dst, load_sem.at[k])
        for k, (src, dst) in enumerate(((emb_hbm, emb), (dir_hbm, direction), (res_hbm, residual)))
    ]
    for load in loads:
        load.start()

    barrier = pltpu.get_barrier_semaphore()
    partners = [beside] + column + layer
    for other in partners:
        pl.semaphore_signal(barrier, inc=1, device_id=(other,), device_id_type=MESH)

    def send(src, dst, send_sem, recv_sem, other):
        return pltpu.make_async_remote_copy(
            src_ref=src, dst_ref=dst, send_sem=send_sem, recv_sem=recv_sem,
            device_id=(other,), device_id_type=MESH,
        )

    def rows_of(k):
        return pl.ds(k * CHUNK, CHUNK)

    far_copies = [
        send(own.at[rows_of(k)], far.at[rows_of(k)], far_send.at[k], far_recv.at[k], opposite)
        for k in range(CHUNKS)
    ]
    near_copies = [
        [
            send(own.at[rows_of(k)], near.at[n, rows_of(k)], near_send.at[n, k], near_recv.at[n, k], other)
            for k in range(CHUNKS)
        ]
        for n, other in enumerate((twin, beside))
    ]
    far_meta_copy = send(own_meta, far_meta, far_meta_send, far_meta_recv, opposite)
    near_meta_copies = [
        send(own_meta, near_meta.at[n], near_meta_send.at[n], near_meta_recv.at[n], other)
        for n, other in enumerate((twin, beside))
    ]
    ret_copies = [
        send(ret_out.at[k], ret_in.at[k], ret_send.at[k], ret_recv.at[k], opposite)
        for k in range(CHUNKS)
    ]

    loads[0].wait()
    loads[1].wait()
    for k in range(CHUNKS):
        rows = rows_of(k)
        scaled = (emb[rows, :].astype(f32) * scale_ref[...]).astype(bf16)
        own[rows, :F] = scaled
        own[rows, F:] = direction[rows, :].astype(bf16)
        wide = scaled.astype(f32)
        left[rows, :] = (-2.0 * wide).astype(bf16)
        norm_col[rows, :] = jnp.broadcast_to(jnp.sum(wide * wide, axis=1, keepdims=True), (CHUNK, 128))
        if k == 0:
            pl.semaphore_wait(barrier, len(partners))

        @pl.when(sends)
        def _():
            far_copies[k].start()

        near_copies[0][k].start()
        near_copies[1][k].start()
    own_meta[0:1, :] = norm_col[...].T[0:1, :]
    own_meta[1:2, :] = ids_ref[...].astype(f32)

    @pl.when(sends)
    def _():
        far_meta_copy.start()

    for copy in near_meta_copies:
        copy.start()

    def add_block(block, meta):
        def some_rows(t, carry):
            rows = pl.ds(pl.multiple_of(t * CHUNK, CHUNK), CHUNK)
            tile = matern(left[rows, :], block[:, :F], norm_col[rows, 0:1], meta[0:1, :])
            acc[rows, :] += dot(tile, block[:, F:])
            return carry

        lax.fori_loop(0, CHUNKS, some_rows, 0)
        return dot(one_hot(meta[1:2, :]), block[:, F:])

    acc[...] = noise_ref[...] * direction[...]
    dir_t[...] = direction[...].T.astype(bf16)
    own_totals = add_block(own, own_meta)
    totals[...] = own_totals
    own_halves_t = split_halves(own_totals).astype(f32).T.astype(bf16)

    near_meta_copies[0].wait_recv()
    for copy in near_copies[0]:
        copy.wait_recv()
    totals[...] += add_block(near.at[0], near_meta.at[0])

    def far_chunk(k):
        far_copies[k].wait_recv()
        rows = rows_of(k)
        tile = matern(left[...], far[rows, :F], norm_col[:, 0:1], far_meta[0:1, rows])
        spots = one_hot(far_meta[1:2, rows])
        back = dot(dir_t[...], tile) + site_weight * dot(own_halves_t, spots)
        ret_out[k] = back.astype(bf16)
        ret_copies[k].start()
        acc[...] += dot(tile, far[rows, F:])
        totals[...] += dot(spots, far[rows, F:])

    def take_back(k):
        ret_copies[k].wait_recv()
        acc[rows_of(k), :] += ret_in[k].astype(f32).T

    @pl.when(receives)
    def _():
        far_meta_copy.wait_recv()
        far_chunk(0)

    near_meta_copies[1].wait_recv()
    for copy in near_copies[1]:
        copy.wait_recv()
    totals[...] += add_block(near.at[1], near_meta.at[1])

    loads[2].wait()
    sums_ref[0:1, :] = jnp.sum(residual[...] * residual[...], axis=0, keepdims=True)

    @pl.when(receives)
    def _():
        for k in range(1, CHUNKS):
            far_chunk(k)

    @pl.when(sends)
    def _():
        for k in range(CHUNKS):
            take_back(k)

    spread = one_hot(own_meta[1:2, :]).astype(f32).T.astype(bf16)
    applied = acc[...] + site_weight * dot(spread, split_halves(totals[...]))
    applied_ref[...] = applied
    sums_ref[1:2, :] = jnp.sum(direction[...] * applied, axis=0, keepdims=True)
    sums_ref[2:3, :] = jnp.sum(residual[...] * applied, axis=0, keepdims=True)
    sums_ref[3:4, :] = jnp.sum(applied * applied, axis=0, keepdims=True)

    def gather_sum(stage, slots, place, others):
        slots[place] = sums_ref[...]
        for other in others:
            send(slots.at[place], slots.at[place], sum_send.at[stage], sum_recv.at[stage], other).start()
        rest = slots.at[pl.ds(0, len(others))]
        every = send(rest, rest, sum_send.at[stage], sum_recv.at[stage], others[0])
        every.wait_recv()
        sums_ref[...] = jnp.sum(slots[...], axis=0)
        return every

    stages = [gather_sum(0, first, column_place, column), gather_sum(1, second, spot, layer)]
    for stage in stages:
        stage.wait_send()

    @pl.when(sends)
    def _():
        far_meta_copy.wait_send()
        for copy in far_copies:
            copy.wait_send()

    @pl.when(receives)
    def _():
        for copy in ret_copies:
            copy.wait_send()

    for copy in near_meta_copies + near_copies[0] + near_copies[1]:
        copy.wait_send()


def body(embeddings, site_ids, inv_scale, noise, solution, residual, direction):
    vmem = pl.BlockSpec(memory_space=pltpu.VMEM)
    anywhere = pl.BlockSpec(memory_space=pl.ANY)
    dma = pltpu.SemaphoreType.DMA
    applied, sums = pl.pallas_call(
        kernel,
        out_shape=(
            jax.ShapeDtypeStruct((ROWS, R), f32),
            jax.ShapeDtypeStruct((4, R), f32),
        ),
        in_specs=[anywhere] * 3 + [vmem] * 3,
        out_specs=[vmem] * 2,
        scratch_shapes=[
            pltpu.VMEM((ROWS, F), bf16),
            pltpu.VMEM((ROWS, R), f32),
            pltpu.VMEM((ROWS, R), f32),
            pltpu.VMEM((ROWS, F + R), bf16),
            pltpu.VMEM((ROWS, F), bf16),
            pltpu.VMEM((ROWS, 128), f32),
            pltpu.VMEM((R, ROWS), bf16),
            pltpu.VMEM((2, ROWS), f32),
            pltpu.VMEM((2, ROWS, F + R), bf16),
            pltpu.VMEM((2, 2, ROWS), f32),
            pltpu.VMEM((ROWS, F + R), bf16),
            pltpu.VMEM((2, ROWS), f32),
            pltpu.VMEM((CHUNKS, R, CHUNK), bf16),
            pltpu.VMEM((CHUNKS, R, CHUNK), bf16),
            pltpu.VMEM((ROWS, R), f32),
            pltpu.VMEM((2 * sites, R), f32),
            pltpu.VMEM((ZS * CS, 4, R), f32),
            pltpu.VMEM((YS * XS, 4, R), f32),
            dma((3,)),
            dma((2, CHUNKS)),
            dma((2, CHUNKS)),
            dma((2,)),
            dma((2,)),
            dma((CHUNKS,)),
            dma((CHUNKS,)),
            dma,
            dma,
            dma((CHUNKS,)),
            dma((CHUNKS,)),
            dma((2,)),
            dma((2,)),
        ],
        compiler_params=pltpu.CompilerParams(
            collective_id=0, has_side_effects=True, vmem_limit_bytes=48 * 1024 * 1024
        ),
        name="cg_products",
    )(embeddings, direction, residual, site_ids.reshape(1, ROWS), inv_scale.reshape(1, F), noise.reshape(1, R))
    old_norms, curvature, mixed, applied_norms = sums
    step_size = old_norms / curvature
    new_norms = jnp.maximum(old_norms - 2.0 * step_size * mixed + step_size * step_size * applied_norms, 0.0)
    new_solution = solution + step_size * direction
    new_residual = residual - step_size * applied
    new_direction = new_residual + new_norms / old_norms * direction
    return (new_solution, new_residual, new_direction, new_norms)


def solution(mesh):
    placed = (P("pts", None), P("pts"), P(), P(), P("pts", None), P("pts", None), P("pts", None))
    return jax.shard_map(
        body,
        mesh=mesh,
        in_specs=placed,
        out_specs=(P("pts", None), P("pts", None), P("pts", None), P()),
        check_vma=False,
    )
```

```python
import functools
import math

import jax
import jax.numpy as jnp
from jax import lax
from jax.experimental import pallas as pl
from jax.experimental.pallas import tpu as pltpu
from jax.sharding import PartitionSpec as P

root_three = math.sqrt(3.0)
site_weight = 0.5
sites = 64

MESH = pl.DeviceIdType.MESH
ZS, YS, XS, CS = 8, 4, 4, 2
PLANE = YS * XS * CS
PTS = ZS * PLANE
ROWS = 1024
F = 384
R = 128
CHUNK = 256
CHUNKS = ROWS // CHUNK
SPOTS = YS * XS
PIECE = ROWS // SPOTS
f32 = jnp.float32
bf16 = jnp.bfloat16


def dot(a, b):
    return jnp.dot(a, b, preferred_element_type=f32)


def matern(left, right, left_norms, right_norms):
    cross = lax.dot_general(left, right, (((1,), (1,)), ((), ())), preferred_element_type=f32)
    squared = jnp.maximum(cross + left_norms + right_norms, 1e-30)
    distance = squared * lax.rsqrt(squared)
    decay = jnp.exp2(distance * (-root_three * math.log2(math.e)))
    return ((1.0 + root_three * distance) * decay).astype(bf16)


def one_hot(ids):
    rows = lax.broadcasted_iota(jnp.int32, (2 * sites, ids.shape[1]), 0) % sites
    return (rows.astype(f32) == ids).astype(bf16)


def split_halves(totals):
    high = totals.astype(bf16)
    low = (totals - high.astype(f32)).astype(bf16)
    rows = lax.broadcasted_iota(jnp.int32, totals.shape, 0)
    return jnp.where(rows < sites, high, low)


def kernel(
    emb_hbm, dir_hbm, res_hbm, ids_hbm, scale_hbm, noise_hbm,
    applied_ref, sums_ref,
    emb, direction, residual, ids_ref, scale_ref, noise_ref, own, left, norm_col, dir_t, own_meta,
    near, near_meta, relay, far, far_meta, ret_out, ret_in, acc, totals, first, second,
    load_sem, near_send, near_recv, near_meta_send, near_meta_recv,
    relay_send, relay_recv, far_send, far_recv, far_meta_send, far_meta_recv,
    ret_send, ret_recv, sum_send, sum_recv,
):
    me = lax.axis_index("pts")
    core = me % CS
    plane = me // PLANE
    spot = (me // CS) % SPOTS
    place = spot + core * (SPOTS - 1 - 2 * spot)
    at_edge = place == 0

    twin = me + 1 - 2 * core
    step = 2 * core - 1
    beside = (me + step + PTS) % PTS
    opposite = (me + PTS // 2) % PTS
    sends = (me // (PTS // 2) + me) % 2 == 0
    receives = jnp.logical_not(sends)
    next_plane = ((plane + step + ZS) % ZS) * PLANE

    def at_place(base, p, c):
        return base + (p + c * (SPOTS - 1 - 2 * p)) * CS + c

    relays = [at_place(next_plane, p, 1 - core) for p in range(SPOTS)]
    next_edge = relays[0]
    own_edge = at_place(plane * PLANE, 0, core)

    column_place = plane * CS + core
    column = [
        ((plane + dz) % ZS) * PLANE + spot * CS + (core + dc) % CS
        for dz in range(ZS) for dc in range(CS) if dz or dc
    ]
    layer = [
        plane * PLANE + ((spot + k) % SPOTS) * CS + core for k in range(1, SPOTS)
    ]

    loads = [
        pltpu.make_async_copy(src, dst, load_sem.at[k])
        for k, (src, dst) in enumerate(
            (
                (emb_hbm, emb), (dir_hbm, direction), (scale_hbm, scale_ref),
                (ids_hbm, ids_ref), (noise_hbm, noise_ref), (res_hbm, residual),
            )
        )
    ]
    for load in loads:
        load.start()

    barrier = pltpu.get_barrier_semaphore()
    partners = [beside] + column + layer
    for other in partners:
        pl.semaphore_signal(barrier, inc=1, device_id=(other,), device_id_type=MESH)

    @pl.when(jnp.logical_not(at_edge))
    def _():
        pl.semaphore_signal(barrier, inc=1, device_id=(next_edge,), device_id_type=MESH)

    def send(src, dst, send_sem, recv_sem, other):
        return pltpu.make_async_remote_copy(
            src_ref=src, dst_ref=dst, send_sem=send_sem, recv_sem=recv_sem,
            device_id=(other,), device_id_type=MESH,
        )

    def rows_of(k):
        return pl.ds(k * CHUNK, CHUNK)

    far_copies = [
        send(own.at[rows_of(k)], far.at[rows_of(k)], far_send.at[k], far_recv.at[k], opposite)
        for k in range(CHUNKS)
    ]
    twin_copies = [
        send(own.at[rows_of(k)], near.at[0, rows_of(k)], near_send.at[0], near_recv.at[0], twin)
        for k in range(CHUNKS)
    ]
    beside_copies = [
        send(own.at[rows_of(k)], near.at[1, rows_of(k)], near_send.at[1], near_recv.at[1], beside)
        for k in range(CHUNKS)
    ]
    near_whole = [
        send(own, near.at[n], near_send.at[n], near_recv.at[n], other)
        for n, other in enumerate((twin, beside))
    ]

    def piece_of(p):
        return pl.ds(p * PIECE, PIECE)

    def edge_copy(p):
        if p == 0:
            return send(own.at[piece_of(0)], near.at[1, piece_of(0)], near_send.at[1], near_recv.at[1], next_edge)
        return send(own.at[piece_of(p)], relay, near_send.at[1], relay_recv, relays[p])

    held_rows = pl.ds(pl.multiple_of(place * PIECE, PIECE), PIECE)
    relay_copy = send(relay, near.at[1, held_rows], relay_send, near_recv.at[1], own_edge)
    relay_in = send(relay, relay, relay_send, relay_recv, own_edge)
    far_meta_copy = send(own_meta, far_meta, far_meta_send, far_meta_recv, opposite)
    near_meta_copies = [
        send(own_meta, near_meta.at[n], near_meta_send.at[n], near_meta_recv.at[n], other)
        for n, other in enumerate((twin, beside))
    ]
    ret_copies = [
        send(ret_out.at[k], ret_in.at[k], ret_send.at[k], ret_recv.at[k], opposite)
        for k in range(CHUNKS)
    ]

    for load in loads[:3]:
        load.wait()
    for k in range(CHUNKS):
        rows = rows_of(k)
        scaled = (emb[rows, :].astype(f32) * scale_ref[...].reshape(1, F)).astype(bf16)
        own[rows, :F] = scaled
        own[rows, F:] = direction[rows, :].astype(bf16)
        wide = scaled.astype(f32)
        left[rows, :] = (-2.0 * wide).astype(bf16)
        norm_col[rows, :] = jnp.broadcast_to(jnp.sum(wide * wide, axis=1, keepdims=True), (CHUNK, 128))
        if k == 0:
            pl.semaphore_wait(barrier, len(partners) + jnp.where(at_edge, SPOTS - 1, 0))

        @pl.when(sends)
        def _():
            far_copies[k].start()

        twin_copies[k].start()

        @pl.when(at_edge)
        def _():
            for p in range(k * CHUNK // PIECE, (k + 1) * CHUNK // PIECE):
                edge_copy(p).start()

        @pl.when(jnp.logical_not(at_edge))
        def _():
            beside_copies[k].start()

    loads[3].wait()
    own_meta[0:1, :] = norm_col[...].T[0:1, :]
    own_meta[1:2, :] = ids_ref[...].reshape(1, ROWS).astype(f32)

    @pl.when(sends)
    def _():
        far_meta_copy.start()

    for copy in near_meta_copies:
        copy.start()

    def add_block(block, meta):
        def some_rows(t, carry):
            rows = pl.ds(pl.multiple_of(t * CHUNK, CHUNK), CHUNK)
            tile = matern(left[rows, :], block[:, :F], norm_col[rows, 0:1], meta[0:1, :])
            acc[rows, :] += dot(tile, block[:, F:])
            return carry

        lax.fori_loop(0, CHUNKS, some_rows, 0)
        return dot(one_hot(meta[1:2, :]), block[:, F:])

    loads[4].wait()
    acc[...] = noise_ref[...].reshape(1, R) * direction[...]
    dir_t[...] = direction[...].T.astype(bf16)
    own_totals = add_block(own, own_meta)
    totals[...] = own_totals
    own_halves_t = split_halves(own_totals).astype(f32).T.astype(bf16)

    near_meta_copies[0].wait_recv()
    near_whole[0].wait_recv()
    totals[...] += add_block(near.at[0], near_meta.at[0])

    @pl.when(jnp.logical_not(at_edge))
    def _():
        relay_in.wait_recv()
        relay_copy.start()

    def far_chunk(k):
        far_copies[k].wait_recv()
        rows = rows_of(k)
        tile = matern(left[...], far[rows, :F], norm_col[:, 0:1], far_meta[0:1, rows])
        spots = one_hot(far_meta[1:2, rows])
        back = dot(dir_t[...], tile) + site_weight * dot(own_halves_t, spots)
        ret_out[k] = back.astype(bf16)
        ret_copies[k].start()
        acc[...] += dot(tile, far[rows, F:])
        totals[...] += dot(spots, far[rows, F:])

    def take_back(k):
        ret_copies[k].wait_recv()
        acc[rows_of(k), :] += ret_in[k].astype(f32).T

    @pl.when(receives)
    def _():
        far_meta_copy.wait_recv()
        far_chunk(0)

    near_meta_copies[1].wait_recv()
    near_whole[1].wait_recv()
    totals[...] += add_block(near.at[1], near_meta.at[1])

    loads[5].wait()
    sums_ref[0:1, :] = jnp.sum(residual[...] * residual[...], axis=0, keepdims=True)

    @pl.when(receives)
    def _():
        for k in range(1, CHUNKS):
            far_chunk(k)

    @pl.when(sends)
    def _():
        for k in range(CHUNKS):
            take_back(k)

    spread = one_hot(own_meta[1:2, :]).astype(f32).T.astype(bf16)
    applied = acc[...] + site_weight * dot(spread, split_halves(totals[...]))
    applied_ref[...] = applied
    sums_ref[1:2, :] = jnp.sum(direction[...] * applied, axis=0, keepdims=True)
    sums_ref[2:3, :] = jnp.sum(residual[...] * applied, axis=0, keepdims=True)
    sums_ref[3:4, :] = jnp.sum(applied * applied, axis=0, keepdims=True)

    def gather_sum(stage, slots, slot, others):
        slots[slot] = sums_ref[...]
        for other in others:
            send(slots.at[slot], slots.at[slot], sum_send.at[stage], sum_recv.at[stage], other).start()
        rest = slots.at[pl.ds(0, len(others))]
        every = send(rest, rest, sum_send.at[stage], sum_recv.at[stage], others[0])
        every.wait_recv()
        sums_ref[...] = jnp.sum(slots[...], axis=0)
        return every

    stages = [gather_sum(0, first, column_place, column), gather_sum(1, second, spot, layer)]
    for stage in stages:
        stage.wait_send()

    @pl.when(sends)
    def _():
        far_meta_copy.wait_send()
        for copy in far_copies:
            copy.wait_send()

    @pl.when(receives)
    def _():
        for copy in ret_copies:
            copy.wait_send()

    @pl.when(jnp.logical_not(at_edge))
    def _():
        relay_copy.wait_send()

    for copy in near_meta_copies + near_whole:
        copy.wait_send()


def body(embeddings, site_ids, inv_scale, noise, solution, residual, direction):
    vmem = pl.BlockSpec(memory_space=pltpu.VMEM)
    hbm = pl.BlockSpec(memory_space=pltpu.HBM)
    dma = pltpu.SemaphoreType.DMA
    applied, sums = pl.pallas_call(
        kernel,
        out_shape=(
            jax.ShapeDtypeStruct((ROWS, R), f32),
            jax.ShapeDtypeStruct((4, R), f32),
        ),
        in_specs=[hbm] * 6,
        out_specs=[vmem] * 2,
        scratch_shapes=[
            pltpu.VMEM((ROWS, F), bf16),
            pltpu.VMEM((ROWS, R), f32),
            pltpu.VMEM((ROWS, R), f32),
            pltpu.VMEM((ROWS,), jnp.int32),
            pltpu.VMEM((F,), f32),
            pltpu.VMEM((R,), f32),
            pltpu.VMEM((ROWS, F + R), bf16),
            pltpu.VMEM((ROWS, F), bf16),
            pltpu.VMEM((ROWS, 128), f32),
            pltpu.VMEM((R, ROWS), bf16),
            pltpu.VMEM((2, ROWS), f32),
            pltpu.VMEM((2, ROWS, F + R), bf16),
            pltpu.VMEM((2, 2, ROWS), f32),
            pltpu.VMEM((PIECE, F + R), bf16),
            pltpu.VMEM((ROWS, F + R), bf16),
            pltpu.VMEM((2, ROWS), f32),
            pltpu.VMEM((CHUNKS, R, CHUNK), bf16),
            pltpu.VMEM((CHUNKS, R, CHUNK), bf16),
            pltpu.VMEM((ROWS, R), f32),
            pltpu.VMEM((2 * sites, R), f32),
            pltpu.VMEM((ZS * CS, 4, R), f32),
            pltpu.VMEM((SPOTS, 4, R), f32),
            dma((6,)),
            dma((2,)),
            dma((2,)),
            dma((2,)),
            dma((2,)),
            dma,
            dma,
            dma((CHUNKS,)),
            dma((CHUNKS,)),
            dma,
            dma,
            dma((CHUNKS,)),
            dma((CHUNKS,)),
            dma((2,)),
            dma((2,)),
        ],
        compiler_params=pltpu.CompilerParams(
            collective_id=0, has_side_effects=True, vmem_limit_bytes=56 * 1024 * 1024
        ),
        name="cg_products",
    )(embeddings, direction, residual, site_ids, inv_scale, noise)
    old_norms, curvature, mixed, applied_norms = sums
    step_size = old_norms / curvature
    new_norms = jnp.maximum(old_norms - 2.0 * step_size * mixed + step_size * step_size * applied_norms, 0.0)
    new_solution = solution + step_size * direction
    new_residual = residual - step_size * applied
    new_direction = new_residual + new_norms / old_norms * direction
    return (new_solution, new_residual, new_direction, new_norms)


def solution(mesh):
    placed = (P("pts", None), P("pts"), P(), P(), P("pts", None), P("pts", None), P("pts", None))
    return jax.shard_map(
        body,
        mesh=mesh,
        in_specs=placed,
        out_specs=(P("pts", None), P("pts", None), P("pts", None), P()),
        check_vma=False,
    )
```

```python
import functools
import math

import jax
import jax.numpy as jnp
from jax import lax
from jax.experimental import pallas as pl
from jax.experimental.pallas import tpu as pltpu
from jax.sharding import PartitionSpec as P

root_three = math.sqrt(3.0)
site_weight = 0.5
sites = 64

MESH = pl.DeviceIdType.MESH
ZS, YS, XS, CS = 8, 4, 4, 2
PLANE = YS * XS * CS
PTS = ZS * PLANE
ROWS = 1024
F = 384
R = 128
CHUNK = 256
CHUNKS = ROWS // CHUNK
LANES = 128
SPOTS = YS * XS
PIECE = ROWS // SPOTS
PARTS = ((0, 256), (256, 256), (512, 256), (768, 128), (896, 128))
f32 = jnp.float32
bf16 = jnp.bfloat16


def dot(a, b):
    return jnp.dot(a, b, preferred_element_type=f32)


def matern(left, right, left_norms, right_norms):
    cross = lax.dot_general(left, right, (((1,), (1,)), ((), ())), preferred_element_type=f32)
    squared = jnp.maximum(cross + left_norms + right_norms, 1e-30)
    distance = squared * lax.rsqrt(squared)
    decay = jnp.exp2(distance * (-root_three * math.log2(math.e)))
    return ((1.0 + root_three * distance) * decay).astype(bf16)


def one_hot(ids):
    rows = lax.broadcasted_iota(jnp.int32, (2 * sites, ids.shape[1]), 0) % sites
    return (rows.astype(f32) == ids).astype(bf16)


def split_halves(totals):
    high = totals.astype(bf16)
    low = (totals - high.astype(f32)).astype(bf16)
    rows = lax.broadcasted_iota(jnp.int32, totals.shape, 0)
    return jnp.where(rows < sites, high, low)


def kernel(
    emb_hbm, dir_hbm, res_hbm, ids_hbm, scale_hbm, noise_hbm,
    applied_hbm, coef_hbm,
    emb, direction, residual, ids_ref, scale_ref, noise_ref, own, left, norm_col, dir_t, own_meta,
    near, near_meta, relay, far, far_meta, ret_out, ret_in, acc, totals, sums_ref, coef_ref, first, second,
    load_sem, near_send, near_recv, near_meta_send, near_meta_recv,
    relay_send, relay_recv, far_send, far_recv, far_meta_send, far_meta_recv,
    ret_send, ret_recv, sum_send, sum_recv, out_sem, coef_sem,
):
    me = lax.axis_index("pts")
    core = me % CS
    plane = me // PLANE
    spot = (me // CS) % SPOTS
    place = spot + core * (SPOTS - 1 - 2 * spot)
    at_edge = place == 0

    twin = me + 1 - 2 * core
    step = 2 * core - 1
    beside = (me + step + PTS) % PTS
    opposite = (me + PTS // 2) % PTS
    sends = (me // (PTS // 2) + me) % 2 == 0
    receives = jnp.logical_not(sends)
    next_plane = ((plane + step + ZS) % ZS) * PLANE

    def at_place(base, p, c):
        return base + (p + c * (SPOTS - 1 - 2 * p)) * CS + c

    relays = [at_place(plane * PLANE, p, core) for p in range(SPOTS)]
    next_relays = [at_place(next_plane, p, 1 - core) for p in range(SPOTS)]
    own_edge, next_edge = relays[0], next_relays[0]

    column_place = plane * CS + core
    column = [
        ((plane + dz) % ZS) * PLANE + spot * CS + (core + dc) % CS
        for dz in range(ZS) for dc in range(CS) if dz or dc
    ]
    layer = [
        plane * PLANE + ((spot + k) % SPOTS) * CS + core for k in range(1, SPOTS)
    ]

    def load(k, src, dst):
        copy = pltpu.make_async_copy(src, dst, load_sem.at[k])
        copy.start()
        return copy

    scale_load = load(0, scale_hbm, scale_ref)
    block_loads = []
    for k in range(CHUNKS):
        rows = pl.ds(k * CHUNK, CHUNK)
        block_loads.append(
            (
                load(4 + 2 * k, emb_hbm.at[rows], emb.at[rows]),
                load(5 + 2 * k, dir_hbm.at[rows], direction.at[rows]),
            )
        )
    ids_load = load(1, ids_hbm, ids_ref)
    noise_load = load(2, noise_hbm, noise_ref)
    res_load = load(3, res_hbm, residual)

    barrier = pltpu.get_barrier_semaphore()
    partners = [beside] + column + layer
    for other in partners:
        pl.semaphore_signal(barrier, inc=1, device_id=(other,), device_id_type=MESH)

    @pl.when(at_edge)
    def _():
        for other in next_relays[1:]:
            pl.semaphore_signal(barrier, inc=1, device_id=(other,), device_id_type=MESH)

    def send(src, dst, send_sem, recv_sem, other):
        return pltpu.make_async_remote_copy(
            src_ref=src, dst_ref=dst, send_sem=send_sem, recv_sem=recv_sem,
            device_id=(other,), device_id_type=MESH,
        )

    def rows_of(k):
        return pl.ds(k * CHUNK, CHUNK)

    far_copies = [
        send(
            own.at[pl.ds(first_row, size)], far.at[pl.ds(first_row, size)],
            far_send.at[k], far_recv.at[k], opposite,
        )
        for k, (first_row, size) in enumerate(PARTS)
    ]
    twin_copies = [
        send(own.at[rows_of(k)], near.at[0, rows_of(k)], near_send.at[0], near_recv.at[0], twin)
        for k in range(CHUNKS)
    ]
    beside_copies = [
        send(own.at[rows_of(k)], near.at[1, rows_of(k)], near_send.at[1], near_recv.at[1], beside)
        for k in range(CHUNKS)
    ]
    near_whole = [
        send(own, near.at[n], near_send.at[n], near_recv.at[n], other)
        for n, other in enumerate((twin, beside))
    ]

    def piece_of(p):
        return pl.ds(p * PIECE, PIECE)

    def edge_copy(p):
        if p == 0:
            return send(own.at[piece_of(0)], near.at[1, piece_of(0)], near_send.at[1], near_recv.at[1], next_edge)
        return send(own.at[piece_of(p)], relay, near_send.at[1], relay_recv, relays[p])

    held_rows = pl.ds(pl.multiple_of(place * PIECE, PIECE), PIECE)
    relay_copy = send(relay, near.at[1, held_rows], relay_send, near_recv.at[1], next_edge)
    relay_in = send(relay, relay, relay_send, relay_recv, own_edge)
    far_meta_copy = send(own_meta, far_meta, far_meta_send, far_meta_recv, opposite)
    near_meta_copies = [
        send(own_meta, near_meta.at[n], near_meta_send.at[n], near_meta_recv.at[n], other)
        for n, other in enumerate((twin, beside))
    ]
    def strips_of(first_row, size):
        return pl.ds(first_row // LANES, size // LANES)

    ret_copies = [
        send(
            ret_out.at[strips_of(*part)], ret_in.at[strips_of(*part)],
            ret_send.at[k], ret_recv.at[k], opposite,
        )
        for k, part in enumerate(PARTS)
    ]

    scale_load.wait()
    for k in range(CHUNKS):
        rows = rows_of(k)
        for copy in block_loads[k]:
            copy.wait()
        own[rows, :F] = (emb[rows, :].astype(f32) * scale_ref[...].reshape(1, F)).astype(bf16)
        own[rows, F:] = direction[rows, :].astype(bf16)
        if k == 0:
            pl.semaphore_wait(barrier, len(partners) + jnp.where(at_edge, 0, 1))

        @pl.when(sends)
        def _():
            for part, copy in zip(PARTS, far_copies):
                if part[0] // CHUNK == k:
                    copy.start()

        @pl.when(at_edge)
        def _():
            for p in range(k * CHUNK // PIECE, (k + 1) * CHUNK // PIECE):
                edge_copy(p).start()

        @pl.when(jnp.logical_not(at_edge))
        def _():
            beside_copies[k].start()

        twin_copies[k].start()

    for k in range(CHUNKS):
        rows = rows_of(k)
        wide = own[rows, :F].astype(f32)
        left[rows, :] = (-2.0 * wide).astype(bf16)
        norm_col[rows, :] = jnp.broadcast_to(jnp.sum(wide * wide, axis=1, keepdims=True), (CHUNK, LANES))
    ids_load.wait()
    own_meta[0:1, :] = norm_col[...].T[0:1, :]
    own_meta[1:2, :] = ids_ref[...].reshape(1, ROWS).astype(f32)

    @pl.when(sends)
    def _():
        far_meta_copy.start()

    for copy in near_meta_copies:
        copy.start()

    def add_block(block, meta):
        def some_rows(t, carry):
            rows = pl.ds(pl.multiple_of(t * CHUNK, CHUNK), CHUNK)
            tile = matern(left[rows, :], block[:, :F], norm_col[rows, 0:1], meta[0:1, :])
            acc[rows, :] += dot(tile, block[:, F:])
            return carry

        lax.fori_loop(0, CHUNKS, some_rows, 0)
        return dot(one_hot(meta[1:2, :]), block[:, F:])

    noise_load.wait()
    acc[...] = noise_ref[...].reshape(1, R) * direction[...]
    dir_t[...] = direction[...].T.astype(bf16)
    own_totals = add_block(own, own_meta)
    totals[...] = own_totals
    own_halves_t = split_halves(own_totals).astype(f32).T.astype(bf16)

    near_meta_copies[0].wait_recv()
    near_whole[0].wait_recv()
    totals[...] += add_block(near.at[0], near_meta.at[0])

    @pl.when(jnp.logical_not(at_edge))
    def _():
        relay_in.wait_recv()
        relay_copy.start()

    def far_part(k):
        far_copies[k].wait_recv()
        first_row, size = PARTS[k]
        rows = pl.ds(first_row, size)
        tile = matern(left[...], far[rows, :F], norm_col[:, 0:1], far_meta[0:1, rows])
        spots = one_hot(far_meta[1:2, rows])
        back = dot(dir_t[...], tile) + site_weight * dot(own_halves_t, spots)
        for strip in range(size // LANES):
            ret_out[first_row // LANES + strip] = back[:, strip * LANES:(strip + 1) * LANES].astype(bf16)
        ret_copies[k].start()
        acc[...] += dot(tile, far[rows, F:])
        totals[...] += dot(spots, far[rows, F:])

    def finish_rows(rows, size):
        spread = one_hot(own_meta[1:2, rows]).astype(f32).T.astype(bf16)
        applied = acc[rows, :] + site_weight * dot(spread, split_halves(totals[...]))
        acc[rows, :] = applied
        held, step_rows = residual[rows, :], direction[rows, :]
        sums_ref[1:2, :] += jnp.sum(step_rows * applied, axis=0, keepdims=True)
        sums_ref[2:3, :] += jnp.sum(held * applied, axis=0, keepdims=True)
        sums_ref[3:4, :] += jnp.sum(applied * applied, axis=0, keepdims=True)
        return pltpu.make_async_copy(acc.at[rows], applied_hbm.at[rows], out_sem)

    @pl.when(receives)
    def _():
        far_meta_copy.wait_recv()
        far_part(0)

    near_meta_copies[1].wait_recv()
    near_whole[1].wait_recv()
    totals[...] += add_block(near.at[1], near_meta.at[1])

    res_load.wait()
    sums_ref[...] = jnp.zeros_like(sums_ref)
    sums_ref[0:1, :] = jnp.sum(residual[...] * residual[...], axis=0, keepdims=True)

    @pl.when(receives)
    def _():
        for k in range(1, len(PARTS)):
            far_part(k)
        finish_rows(pl.ds(0, ROWS), ROWS).start()

    @pl.when(sends)
    def _():
        for k, (first_row, size) in enumerate(PARTS):
            ret_copies[k].wait_recv()
            for strip in range(first_row // LANES, (first_row + size) // LANES):
                acc[pl.ds(strip * LANES, LANES), :] += ret_in[strip].astype(f32).T
            finish_rows(pl.ds(first_row, size), size).start()

    def gather_sum(stage, slots, slot, others):
        slots[slot] = sums_ref[...]
        for other in others:
            send(slots.at[slot], slots.at[slot], sum_send.at[stage], sum_recv.at[stage], other).start()
        rest = slots.at[pl.ds(0, len(others))]
        every = send(rest, rest, sum_send.at[stage], sum_recv.at[stage], others[0])
        every.wait_recv()
        sums_ref[...] = jnp.sum(slots[...], axis=0)
        return every

    stages = [gather_sum(0, first, column_place, column), gather_sum(1, second, spot, layer)]
    old_norms, curvature = sums_ref[0:1, :], sums_ref[1:2, :]
    step_size = old_norms / curvature
    new_norms = old_norms - 2.0 * step_size * sums_ref[2:3, :] + step_size * step_size * sums_ref[3:4, :]
    new_norms = jnp.maximum(new_norms, 0.0)
    coef_ref[0:1, :] = step_size
    coef_ref[1:2, :] = new_norms / old_norms
    coef_ref[2:3, :] = new_norms
    coef_ref[3:4, :] = old_norms
    coef_out = pltpu.make_async_copy(coef_ref, coef_hbm, coef_sem)
    coef_out.start()
    for stage in stages:
        stage.wait_send()

    @pl.when(sends)
    def _():
        far_meta_copy.wait_send()
        for copy in far_copies:
            copy.wait_send()

    @pl.when(receives)
    def _():
        for copy in ret_copies:
            copy.wait_send()

    @pl.when(jnp.logical_not(at_edge))
    def _():
        relay_copy.wait_send()

    for copy in near_meta_copies + near_whole:
        copy.wait_send()
    pltpu.make_async_copy(acc, applied_hbm, out_sem).wait()
    coef_out.wait()


def update(
    sol_hbm, res_hbm, dir_hbm, applied_hbm, coef_hbm,
    new_sol_hbm, new_res_hbm, new_dir_hbm, norms_hbm,
    coef_ref, held, made, norms, in_sem, out_sem,
):
    def copy(src, dst, sem):
        moving = pltpu.make_async_copy(src, dst, sem)
        moving.start()
        return moving

    coef_in = copy(coef_hbm, coef_ref, in_sem.at[4 * CHUNKS])
    loads, stores = [], []
    for k in range(CHUNKS):
        rows = pl.ds(k * CHUNK, CHUNK)
        for n, src in enumerate((applied_hbm, res_hbm, dir_hbm, sol_hbm)):
            loads.append(copy(src.at[rows], held.at[n, rows], in_sem.at[4 * k + n]))
    coef_in.wait()
    step_size, ratio = coef_ref[0:1, :], coef_ref[1:2, :]
    norms[...] = coef_ref[2:3, :].reshape(R)
    stores.append(copy(norms, norms_hbm, out_sem.at[3 * CHUNKS]))
    for k in range(CHUNKS):
        rows = pl.ds(k * CHUNK, CHUNK)
        for n in range(4):
            loads[4 * k + n].wait()
        step_rows = held[2, rows, :]
        moved = held[1, rows, :] - step_size * held[0, rows, :]
        made[0, rows, :] = moved
        made[1, rows, :] = held[3, rows, :] + step_size * step_rows
        made[2, rows, :] = moved + ratio * step_rows
        for n, out in enumerate((new_res_hbm, new_sol_hbm, new_dir_hbm)):
            stores.append(copy(made.at[n, rows], out.at[rows], out_sem.at[3 * k + n]))
    for store in stores:
        store.wait()


def body(embeddings, site_ids, inv_scale, noise, solution, residual, direction):
    hbm = pl.BlockSpec(memory_space=pltpu.HBM)
    dma = pltpu.SemaphoreType.DMA
    applied, coefs = pl.pallas_call(
        kernel,
        out_shape=(
            jax.ShapeDtypeStruct((ROWS, R), f32),
            jax.ShapeDtypeStruct((4, R), f32),
        ),
        in_specs=[hbm] * 6,
        out_specs=[hbm] * 2,
        scratch_shapes=[
            pltpu.VMEM((ROWS, F), bf16),
            pltpu.VMEM((ROWS, R), f32),
            pltpu.VMEM((ROWS, R), f32),
            pltpu.VMEM((ROWS,), jnp.int32),
            pltpu.VMEM((F,), f32),
            pltpu.VMEM((R,), f32),
            pltpu.VMEM((ROWS, F + R), bf16),
            pltpu.VMEM((ROWS, F), bf16),
            pltpu.VMEM((ROWS, 128), f32),
            pltpu.VMEM((R, ROWS), bf16),
            pltpu.VMEM((2, ROWS), f32),
            pltpu.VMEM((2, ROWS, F + R), bf16),
            pltpu.VMEM((2, 2, ROWS), f32),
            pltpu.VMEM((PIECE, F + R), bf16),
            pltpu.VMEM((ROWS, F + R), bf16),
            pltpu.VMEM((2, ROWS), f32),
            pltpu.VMEM((ROWS // LANES, R, LANES), bf16),
            pltpu.VMEM((ROWS // LANES, R, LANES), bf16),
            pltpu.VMEM((ROWS, R), f32),
            pltpu.VMEM((2 * sites, R), f32),
            pltpu.VMEM((4, R), f32),
            pltpu.VMEM((4, R), f32),
            pltpu.VMEM((ZS * CS, 4, R), f32),
            pltpu.VMEM((SPOTS, 4, R), f32),
            dma((4 + 2 * CHUNKS,)),
            dma((2,)),
            dma((2,)),
            dma((2,)),
            dma((2,)),
            dma,
            dma,
            dma((len(PARTS),)),
            dma((len(PARTS),)),
            dma,
            dma,
            dma((len(PARTS),)),
            dma((len(PARTS),)),
            dma((2,)),
            dma((2,)),
            dma,
            dma,
        ],
        compiler_params=pltpu.CompilerParams(
            collective_id=0, has_side_effects=True, vmem_limit_bytes=56 * 1024 * 1024
        ),
        name="cg_products",
    )(embeddings, direction, residual, site_ids, inv_scale, noise)
    block = jax.ShapeDtypeStruct((ROWS, R), f32)
    new_solution, new_residual, new_direction, new_norms = pl.pallas_call(
        update,
        out_shape=(block, block, block, jax.ShapeDtypeStruct((R,), f32)),
        in_specs=[hbm] * 5,
        out_specs=[hbm] * 4,
        scratch_shapes=[
            pltpu.VMEM((4, R), f32),
            pltpu.VMEM((4, ROWS, R), f32),
            pltpu.VMEM((3, ROWS, R), f32),
            pltpu.VMEM((R,), f32),
            dma((4 * CHUNKS + 1,)),
            dma((3 * CHUNKS + 1,)),
        ],
        compiler_params=pltpu.CompilerParams(vmem_limit_bytes=62 * 1024 * 1024),
        name="cg_update",
    )(solution, residual, direction, applied, coefs)
    return (new_solution, new_residual, new_direction, new_norms)


def solution(mesh):
    placed = (P("pts", None), P("pts"), P(), P(), P("pts", None), P("pts", None), P("pts", None))
    return jax.shard_map(
        body,
        mesh=mesh,
        in_specs=placed,
        out_specs=(P("pts", None), P("pts", None), P("pts", None), P()),
        check_vma=False,
    )
```

```python
import functools
import math

import jax
import jax.numpy as jnp
from jax import lax
from jax.experimental import pallas as pl
from jax.experimental.pallas import tpu as pltpu
from jax.sharding import PartitionSpec as P

root_three = math.sqrt(3.0)
site_weight = 0.5
sites = 64

MESH = pl.DeviceIdType.MESH
ZS, YS, XS, CS = 8, 4, 4, 2
PLANE = YS * XS * CS
PTS = ZS * PLANE
ROWS = 1024
F = 384
R = 128
CHUNK = 256
CHUNKS = ROWS // CHUNK
LANES = 128
SPOTS = YS * XS
PIECE = ROWS // SPOTS
PARTS = ((0, 256), (256, 256), (512, 256), (768, 128), (896, 128))
f32 = jnp.float32
bf16 = jnp.bfloat16


def dot(a, b):
    return jnp.dot(a, b, preferred_element_type=f32)


def matern(left, right, left_norms, right_norms):
    cross = lax.dot_general(left, right, (((1,), (1,)), ((), ())), preferred_element_type=f32)
    squared = jnp.maximum(cross + left_norms + right_norms, 1e-30)
    distance = squared * lax.rsqrt(squared)
    decay = jnp.exp2(distance * (-root_three * math.log2(math.e)))
    return ((1.0 + root_three * distance) * decay).astype(bf16)


def one_hot(ids):
    rows = lax.broadcasted_iota(jnp.int32, (2 * sites, ids.shape[1]), 0) % sites
    return (rows.astype(f32) == ids).astype(bf16)


def split_halves(totals):
    high = totals.astype(bf16)
    low = (totals - high.astype(f32)).astype(bf16)
    rows = lax.broadcasted_iota(jnp.int32, totals.shape, 0)
    return jnp.where(rows < sites, high, low)


def kernel(
    emb_hbm, dir_hbm, res_hbm, ids_hbm, scale_hbm, noise_hbm,
    acc, direction, residual, coef_ref,
    emb, ids_ref, scale_ref, noise_ref, own, left, norm_col, dir_t, own_meta,
    near, near_meta, relay, far, far_meta, ret_out, ret_in, totals, sums_ref, first, second,
    load_sem, near_send, near_recv, near_meta_send, near_meta_recv,
    relay_send, relay_recv, far_send, far_recv, far_meta_send, far_meta_recv,
    ret_send, ret_recv, sum_send, sum_recv,
):
    me = lax.axis_index("pts")
    core = me % CS
    plane = me // PLANE
    spot = (me // CS) % SPOTS
    place = spot + core * (SPOTS - 1 - 2 * spot)
    at_edge = place == 0

    twin = me + 1 - 2 * core
    step = 2 * core - 1
    beside = (me + step + PTS) % PTS
    opposite = (me + PTS // 2) % PTS
    sends = (me // (PTS // 2) + me) % 2 == 0
    receives = jnp.logical_not(sends)
    next_plane = ((plane + step + ZS) % ZS) * PLANE

    def at_place(base, p, c):
        return base + (p + c * (SPOTS - 1 - 2 * p)) * CS + c

    relays = [at_place(plane * PLANE, p, core) for p in range(SPOTS)]
    next_relays = [at_place(next_plane, p, 1 - core) for p in range(SPOTS)]
    own_edge, next_edge = relays[0], next_relays[0]

    column_place = plane * CS + core
    row, col = spot // XS, spot % XS

    def turn(distance, size):
        return min(distance, size - distance)

    column = [
        ((plane + dz) % ZS) * PLANE + spot * CS + (core + dc) % CS
        for dz in sorted(range(ZS), key=lambda d: -turn(d, ZS)) for dc in range(CS) if dz or dc
    ]
    layer = [
        plane * PLANE + ((row + dy) % YS * XS + (col + dx) % XS) * CS + core
        for dy, dx in sorted(
            ((dy, dx) for dy in range(YS) for dx in range(XS) if dy or dx),
            key=lambda d: -turn(d[0], YS) - turn(d[1], XS),
        )
    ]

    def load(k, src, dst):
        copy = pltpu.make_async_copy(src, dst, load_sem.at[k])
        copy.start()
        return copy

    scale_load = load(0, scale_hbm, scale_ref)
    block_loads = []
    for k in range(CHUNKS):
        rows = pl.ds(k * CHUNK, CHUNK)
        block_loads.append(
            (
                load(4 + 2 * k, emb_hbm.at[rows], emb.at[rows]),
                load(5 + 2 * k, dir_hbm.at[rows], direction.at[rows]),
            )
        )
    ids_load = load(1, ids_hbm, ids_ref)
    noise_load = load(2, noise_hbm, noise_ref)
    res_load = load(3, res_hbm, residual)

    barrier = pltpu.get_barrier_semaphore()
    partners = [other for pair in zip(column, layer) for other in pair] + [beside]
    for other in partners:
        pl.semaphore_signal(barrier, inc=1, device_id=(other,), device_id_type=MESH)

    @pl.when(at_edge)
    def _():
        for other in next_relays[1:]:
            pl.semaphore_signal(barrier, inc=1, device_id=(other,), device_id_type=MESH)

    def send(src, dst, send_sem, recv_sem, other):
        return pltpu.make_async_remote_copy(
            src_ref=src, dst_ref=dst, send_sem=send_sem, recv_sem=recv_sem,
            device_id=(other,), device_id_type=MESH,
        )

    def rows_of(k):
        return pl.ds(k * CHUNK, CHUNK)

    far_copies = [
        send(
            own.at[pl.ds(first_row, size)], far.at[pl.ds(first_row, size)],
            far_send.at[k], far_recv.at[k], opposite,
        )
        for k, (first_row, size) in enumerate(PARTS)
    ]
    twin_copies = [
        send(own.at[rows_of(k)], near.at[0, rows_of(k)], near_send.at[0], near_recv.at[0], twin)
        for k in range(CHUNKS)
    ]
    beside_copies = [
        send(own.at[rows_of(k)], near.at[1, rows_of(k)], near_send.at[1], near_recv.at[1], beside)
        for k in range(CHUNKS)
    ]
    near_whole = [
        send(own, near.at[n], near_send.at[n], near_recv.at[n], other)
        for n, other in enumerate((twin, beside))
    ]

    def piece_of(p):
        return pl.ds(p * PIECE, PIECE)

    def edge_copy(p):
        if p == 0:
            return send(own.at[piece_of(0)], near.at[1, piece_of(0)], near_send.at[1], near_recv.at[1], next_edge)
        return send(own.at[piece_of(p)], relay, near_send.at[1], relay_recv, relays[p])

    held_rows = pl.ds(pl.multiple_of(place * PIECE, PIECE), PIECE)
    relay_copy = send(relay, near.at[1, held_rows], relay_send, near_recv.at[1], next_edge)
    relay_in = send(relay, relay, relay_send, relay_recv, own_edge)
    far_meta_copy = send(own_meta, far_meta, far_meta_send, far_meta_recv, opposite)
    near_meta_copies = [
        send(own_meta, near_meta.at[n], near_meta_send.at[n], near_meta_recv.at[n], other)
        for n, other in enumerate((twin, beside))
    ]
    def strips_of(first_row, size):
        return pl.ds(first_row // LANES, size // LANES)

    ret_copies = [
        send(
            ret_out.at[strips_of(*part)], ret_in.at[strips_of(*part)],
            ret_send.at[k], ret_recv.at[k], opposite,
        )
        for k, part in enumerate(PARTS)
    ]

    scale_load.wait()
    for k in range(CHUNKS):
        rows = rows_of(k)
        for copy in block_loads[k]:
            copy.wait()
        own[rows, :F] = (emb[rows, :].astype(f32) * scale_ref[...].reshape(1, F)).astype(bf16)
        own[rows, F:] = direction[rows, :].astype(bf16)
        if k == 0:
            pl.semaphore_wait(barrier, len(partners) + jnp.where(at_edge, 0, 1))

        @pl.when(sends)
        def _():
            for part, copy in zip(PARTS, far_copies):
                if part[0] // CHUNK == k:
                    copy.start()

        @pl.when(at_edge)
        def _():
            for p in range(k * CHUNK // PIECE, (k + 1) * CHUNK // PIECE):
                edge_copy(p).start()

        @pl.when(jnp.logical_not(at_edge))
        def _():
            beside_copies[k].start()

        twin_copies[k].start()

    for k in range(CHUNKS):
        rows = rows_of(k)
        wide = own[rows, :F].astype(f32)
        left[rows, :] = (-2.0 * wide).astype(bf16)
        norm_col[rows, :] = jnp.broadcast_to(jnp.sum(wide * wide, axis=1, keepdims=True), (CHUNK, LANES))
    ids_load.wait()
    own_meta[0:1, :] = norm_col[...].T[0:1, :]
    own_meta[1:2, :] = ids_ref[...].reshape(1, ROWS).astype(f32)

    @pl.when(sends)
    def _():
        far_meta_copy.start()

    for copy in near_meta_copies:
        copy.start()

    def add_block(block, meta):
        def some_rows(t, carry):
            rows = pl.ds(pl.multiple_of(t * CHUNK, CHUNK), CHUNK)
            tile = matern(left[rows, :], block[:, :F], norm_col[rows, 0:1], meta[0:1, :])
            acc[rows, :] += dot(tile, block[:, F:])
            return carry

        lax.fori_loop(0, CHUNKS, some_rows, 0)
        return dot(one_hot(meta[1:2, :]), block[:, F:])

    noise_load.wait()
    acc[...] = noise_ref[...].reshape(1, R) * direction[...]
    dir_t[...] = direction[...].T.astype(bf16)
    own_totals = add_block(own, own_meta)
    totals[...] = own_totals
    own_halves_t = split_halves(own_totals).astype(f32).T.astype(bf16)

    @pl.when(jnp.logical_not(at_edge))
    def _():
        relay_in.wait_recv()
        relay_copy.start()

    near_meta_copies[0].wait_recv()
    near_whole[0].wait_recv()
    totals[...] += add_block(near.at[0], near_meta.at[0])

    def far_part(k):
        far_copies[k].wait_recv()
        first_row, size = PARTS[k]
        rows = pl.ds(first_row, size)
        tile = matern(left[...], far[rows, :F], norm_col[:, 0:1], far_meta[0:1, rows])
        spots = one_hot(far_meta[1:2, rows])
        back = dot(dir_t[...], tile) + site_weight * dot(own_halves_t, spots)
        for strip in range(size // LANES):
            ret_out[first_row // LANES + strip] = back[:, strip * LANES:(strip + 1) * LANES].astype(bf16)
        ret_copies[k].start()
        acc[...] += dot(tile, far[rows, F:])
        totals[...] += dot(spots, far[rows, F:])

    def finish_rows(rows):
        spread = one_hot(own_meta[1:2, rows]).astype(f32).T.astype(bf16)
        applied = acc[rows, :] + site_weight * dot(spread, split_halves(totals[...]))
        acc[rows, :] = applied
        held, step_rows = residual[rows, :], direction[rows, :]
        sums_ref[1:2, :] += jnp.sum(step_rows * applied, axis=0, keepdims=True)
        sums_ref[2:3, :] += jnp.sum(held * applied, axis=0, keepdims=True)
        sums_ref[3:4, :] += jnp.sum(applied * applied, axis=0, keepdims=True)

    @pl.when(receives)
    def _():
        far_meta_copy.wait_recv()
        far_part(0)
        far_part(1)
        far_part(2)

    near_meta_copies[1].wait_recv()
    near_whole[1].wait_recv()
    totals[...] += add_block(near.at[1], near_meta.at[1])

    res_load.wait()
    sums_ref[...] = jnp.zeros_like(sums_ref)
    sums_ref[0:1, :] = jnp.sum(residual[...] * residual[...], axis=0, keepdims=True)

    @pl.when(receives)
    def _():
        for k in range(3, len(PARTS)):
            far_part(k)
        finish_rows(pl.ds(0, ROWS))

    @pl.when(sends)
    def _():
        for k, (first_row, size) in enumerate(PARTS):
            ret_copies[k].wait_recv()
            for strip in range(first_row // LANES, (first_row + size) // LANES):
                acc[pl.ds(strip * LANES, LANES), :] += ret_in[strip].astype(f32).T
            finish_rows(pl.ds(first_row, size))

    def gather_sum(stage, slots, slot, others):
        slots[slot] = sums_ref[...]
        for other in others:
            send(slots.at[slot], slots.at[slot], sum_send.at[stage], sum_recv.at[stage], other).start()
        rest = slots.at[pl.ds(0, len(others))]
        every = send(rest, rest, sum_send.at[stage], sum_recv.at[stage], others[0])
        every.wait_recv()
        sums_ref[...] = jnp.sum(slots[...], axis=0)
        return every

    stages = [gather_sum(0, first, column_place, column), gather_sum(1, second, spot, layer)]
    old_norms, curvature = sums_ref[0:1, :], sums_ref[1:2, :]
    step_size = old_norms / curvature
    new_norms = old_norms - 2.0 * step_size * sums_ref[2:3, :] + step_size * step_size * sums_ref[3:4, :]
    new_norms = jnp.maximum(new_norms, 0.0)
    coef_ref[0:1, :] = step_size
    coef_ref[1:2, :] = new_norms / old_norms
    coef_ref[2:3, :] = new_norms
    coef_ref[3:4, :] = old_norms
    for stage in stages:
        stage.wait_send()

    @pl.when(sends)
    def _():
        far_meta_copy.wait_send()
        for copy in far_copies:
            copy.wait_send()

    @pl.when(receives)
    def _():
        for copy in ret_copies:
            copy.wait_send()

    @pl.when(jnp.logical_not(at_edge))
    def _():
        relay_copy.wait_send()

    for copy in near_meta_copies + near_whole:
        copy.wait_send()


def update(
    sol_ref, res_ref, dir_ref, applied_ref, coef_ref,
    new_sol_hbm, new_res_hbm, new_dir_hbm, norms_hbm,
    made, norms, out_sem,
):
    stores = []

    def store(src, dst, sem):
        stores.append(pltpu.make_async_copy(src, dst, sem))
        stores[-1].start()

    step_size, ratio = coef_ref[0:1, :], coef_ref[1:2, :]
    norms[...] = coef_ref[2:3, :].reshape(R)
    store(norms, norms_hbm, out_sem.at[3 * CHUNKS])
    for k in range(CHUNKS):
        rows = pl.ds(k * CHUNK, CHUNK)
        step_rows = dir_ref[rows, :]
        moved = res_ref[rows, :] - step_size * applied_ref[rows, :]
        made[0, rows, :] = moved
        made[1, rows, :] = sol_ref[rows, :] + step_size * step_rows
        made[2, rows, :] = moved + ratio * step_rows
        for n, out in enumerate((new_res_hbm, new_sol_hbm, new_dir_hbm)):
            store(made.at[n, rows], out.at[rows], out_sem.at[3 * k + n])
    for copy in stores:
        copy.wait()


def body(embeddings, site_ids, inv_scale, noise, solution, residual, direction):
    hbm = pl.BlockSpec(memory_space=pltpu.HBM)
    vmem = pl.BlockSpec(memory_space=pltpu.VMEM)
    dma = pltpu.SemaphoreType.DMA
    applied, held_direction, held_residual, coefs = pl.pallas_call(
        kernel,
        out_shape=(
            pltpu.VMEM((ROWS, R), f32),
            pltpu.VMEM((ROWS, R), f32),
            pltpu.VMEM((ROWS, R), f32),
            pltpu.VMEM((4, R), f32),
        ),
        in_specs=[hbm] * 6,
        out_specs=[vmem] * 4,
        scratch_shapes=[
            pltpu.VMEM((ROWS, F), bf16),
            pltpu.VMEM((ROWS,), jnp.int32),
            pltpu.VMEM((F,), f32),
            pltpu.VMEM((R,), f32),
            pltpu.VMEM((ROWS, F + R), bf16),
            pltpu.VMEM((ROWS, F), bf16),
            pltpu.VMEM((ROWS, 128), f32),
            pltpu.VMEM((R, ROWS), bf16),
            pltpu.VMEM((2, ROWS), f32),
            pltpu.VMEM((2, ROWS, F + R), bf16),
            pltpu.VMEM((2, 2, ROWS), f32),
            pltpu.VMEM((PIECE, F + R), bf16),
            pltpu.VMEM((ROWS, F + R), bf16),
            pltpu.VMEM((2, ROWS), f32),
            pltpu.VMEM((ROWS // LANES, R, LANES), bf16),
            pltpu.VMEM((ROWS // LANES, R, LANES), bf16),
            pltpu.VMEM((2 * sites, R), f32),
            pltpu.VMEM((4, R), f32),
            pltpu.VMEM((ZS * CS, 4, R), f32),
            pltpu.VMEM((SPOTS, 4, R), f32),
            dma((4 + 2 * CHUNKS,)),
            dma((2,)),
            dma((2,)),
            dma((2,)),
            dma((2,)),
            dma,
            dma,
            dma((len(PARTS),)),
            dma((len(PARTS),)),
            dma,
            dma,
            dma((len(PARTS),)),
            dma((len(PARTS),)),
            dma((2,)),
            dma((2,)),
        ],
        compiler_params=pltpu.CompilerParams(
            collective_id=0, has_side_effects=True, vmem_limit_bytes=56 * 1024 * 1024
        ),
        name="cg_products",
    )(embeddings, direction, residual, site_ids, inv_scale, noise)
    block = jax.ShapeDtypeStruct((ROWS, R), f32)
    new_solution, new_residual, new_direction, new_norms = pl.pallas_call(
        update,
        out_shape=(block, block, block, jax.ShapeDtypeStruct((R,), f32)),
        in_specs=[vmem] * 5,
        out_specs=[hbm] * 4,
        scratch_shapes=[
            pltpu.VMEM((3, ROWS, R), f32),
            pltpu.VMEM((R,), f32),
            dma((3 * CHUNKS + 1,)),
        ],
        compiler_params=pltpu.CompilerParams(vmem_limit_bytes=8 * 1024 * 1024),
        name="cg_update",
    )(solution, held_residual, held_direction, applied, coefs)
    return (new_solution, new_residual, new_direction, new_norms)


def solution(mesh):
    placed = (P("pts", None), P("pts"), P(), P(), P("pts", None), P("pts", None), P("pts", None))
    return jax.shard_map(
        body,
        mesh=mesh,
        in_specs=placed,
        out_specs=(P("pts", None), P("pts", None), P("pts", None), P()),
        check_vma=False,
    )
```

```python
import functools
import math

import jax
import jax.numpy as jnp
from jax import lax
from jax.experimental import pallas as pl
from jax.experimental.pallas import tpu as pltpu
from jax.sharding import PartitionSpec as P

root_three = math.sqrt(3.0)
site_weight = 0.5
sites = 64

MESH = pl.DeviceIdType.MESH
ZS, YS, XS, CS = 8, 4, 4, 2
PLANE = YS * XS * CS
PTS = ZS * PLANE
ROWS = 1024
F = 384
R = 128
CHUNK = 256
CHUNKS = ROWS // CHUNK
LANES = 128
SPOTS = YS * XS
PIECE = ROWS // SPOTS
PARTS = ((0, 256), (256, 256), (512, 256), (768, 128), (896, 128))
f32 = jnp.float32
bf16 = jnp.bfloat16


def dot(a, b):
    return jnp.dot(a, b, preferred_element_type=f32)


def matern(left, right, left_norms, right_norms):
    cross = lax.dot_general(left, right, (((1,), (1,)), ((), ())), preferred_element_type=f32)
    squared = jnp.maximum(cross + left_norms + right_norms, 1e-30)
    distance = squared * lax.rsqrt(squared)
    decay = jnp.exp2(distance * (-root_three * math.log2(math.e)))
    return ((1.0 + root_three * distance) * decay).astype(bf16)


def one_hot(ids):
    rows = lax.broadcasted_iota(jnp.int32, (2 * sites, ids.shape[1]), 0) % sites
    return (rows.astype(f32) == ids).astype(bf16)


def split_halves(totals):
    high = totals.astype(bf16)
    low = (totals - high.astype(f32)).astype(bf16)
    rows = lax.broadcasted_iota(jnp.int32, totals.shape, 0)
    return jnp.where(rows < sites, high, low)


def kernel(
    emb_hbm, dir_hbm, res_hbm, ids_hbm, scale_hbm, noise_hbm,
    acc, direction, residual, coef_ref,
    emb, ids_ref, scale_ref, noise_ref, own, left, norm_col, dir_t, own_meta,
    near, near_meta, relay, far, far_meta, ret_out, ret_in, totals, spread, sums_ref, first, second,
    load_sem, near_send, near_recv, near_meta_send, near_meta_recv,
    relay_send, relay_recv, far_send, far_recv, far_meta_send, far_meta_recv,
    ret_send, ret_recv, sum_send, sum_recv,
):
    me = lax.axis_index("pts")
    core = me % CS
    plane = me // PLANE
    spot = (me // CS) % SPOTS
    place = spot + core * (SPOTS - 1 - 2 * spot)
    at_edge = place == 0

    twin = me + 1 - 2 * core
    step = 2 * core - 1
    beside = (me + step + PTS) % PTS
    opposite = (me + PTS // 2) % PTS
    sends = (me // (PTS // 2) + me) % 2 == 0
    receives = jnp.logical_not(sends)
    next_plane = ((plane + step + ZS) % ZS) * PLANE

    def at_place(base, p, c):
        return base + (p + c * (SPOTS - 1 - 2 * p)) * CS + c

    relays = [at_place(plane * PLANE, p, core) for p in range(SPOTS)]
    next_relays = [at_place(next_plane, p, 1 - core) for p in range(SPOTS)]
    own_edge, next_edge = relays[0], next_relays[0]

    column_place = plane * CS + core
    row, col = spot // XS, spot % XS

    def turn(distance, size):
        return min(distance, size - distance)

    column = [
        ((plane + dz) % ZS) * PLANE + spot * CS + (core + dc) % CS
        for dz in sorted(range(ZS), key=lambda d: -turn(d, ZS)) for dc in range(CS) if dz or dc
    ]
    layer = [
        plane * PLANE + ((row + dy) % YS * XS + (col + dx) % XS) * CS + core
        for dy, dx in sorted(
            ((dy, dx) for dy in range(YS) for dx in range(XS) if dy or dx),
            key=lambda d: -turn(d[0], YS) - turn(d[1], XS),
        )
    ]

    def load(k, src, dst):
        copy = pltpu.make_async_copy(src, dst, load_sem.at[k])
        copy.start()
        return copy

    scale_load = load(0, scale_hbm, scale_ref)
    block_loads = []
    for k in range(CHUNKS):
        rows = pl.ds(k * CHUNK, CHUNK)
        block_loads.append(
            (
                load(4 + 2 * k, emb_hbm.at[rows], emb.at[rows]),
                load(5 + 2 * k, dir_hbm.at[rows], direction.at[rows]),
            )
        )
    ids_load = load(1, ids_hbm, ids_ref)
    noise_load = load(2, noise_hbm, noise_ref)
    res_load = load(3, res_hbm, residual)

    barrier = pltpu.get_barrier_semaphore()
    partners = [other for pair in zip(column, layer) for other in pair] + [beside]
    for other in partners:
        pl.semaphore_signal(barrier, inc=1, device_id=(other,), device_id_type=MESH)

    @pl.when(at_edge)
    def _():
        for other in next_relays[1:]:
            pl.semaphore_signal(barrier, inc=1, device_id=(other,), device_id_type=MESH)

    def send(src, dst, send_sem, recv_sem, other):
        return pltpu.make_async_remote_copy(
            src_ref=src, dst_ref=dst, send_sem=send_sem, recv_sem=recv_sem,
            device_id=(other,), device_id_type=MESH,
        )

    def rows_of(k):
        return pl.ds(k * CHUNK, CHUNK)

    far_copies = [
        send(
            own.at[pl.ds(first_row, size)], far.at[pl.ds(first_row, size)],
            far_send.at[k], far_recv.at[k], opposite,
        )
        for k, (first_row, size) in enumerate(PARTS)
    ]
    twin_copies = [
        send(own.at[rows_of(k)], near.at[0, rows_of(k)], near_send.at[0], near_recv.at[0], twin)
        for k in range(CHUNKS)
    ]
    beside_copies = [
        send(own.at[rows_of(k)], near.at[1, rows_of(k)], near_send.at[1], near_recv.at[1], beside)
        for k in range(CHUNKS)
    ]
    near_whole = [
        send(own, near.at[n], near_send.at[n], near_recv.at[n], other)
        for n, other in enumerate((twin, beside))
    ]

    def piece_of(p):
        return pl.ds(p * PIECE, PIECE)

    def edge_copy(p):
        if p == 0:
            return send(own.at[piece_of(0)], near.at[1, piece_of(0)], near_send.at[1], near_recv.at[1], next_edge)
        return send(own.at[piece_of(p)], relay, near_send.at[1], relay_recv, relays[p])

    held_rows = pl.ds(pl.multiple_of(place * PIECE, PIECE), PIECE)
    relay_copy = send(relay, near.at[1, held_rows], relay_send, near_recv.at[1], next_edge)
    relay_in = send(relay, relay, relay_send, relay_recv, own_edge)
    far_meta_copy = send(own_meta, far_meta, far_meta_send, far_meta_recv, opposite)
    near_meta_copies = [
        send(own_meta, near_meta.at[n], near_meta_send.at[n], near_meta_recv.at[n], other)
        for n, other in enumerate((twin, beside))
    ]
    def strips_of(first_row, size):
        return pl.ds(first_row // LANES, size // LANES)

    ret_copies = [
        send(
            ret_out.at[strips_of(*part)], ret_in.at[strips_of(*part)],
            ret_send.at[k], ret_recv.at[k], opposite,
        )
        for k, part in enumerate(PARTS)
    ]

    scale_load.wait()
    for k in range(CHUNKS):
        rows = rows_of(k)
        for copy in block_loads[k]:
            copy.wait()
        own[rows, :F] = (emb[rows, :].astype(f32) * scale_ref[...].reshape(1, F)).astype(bf16)
        own[rows, F:] = direction[rows, :].astype(bf16)
        if k == 0:
            pl.semaphore_wait(barrier, len(partners) + jnp.where(at_edge, 0, 1))

        @pl.when(sends)
        def _():
            for part, copy in zip(PARTS, far_copies):
                if part[0] // CHUNK == k:
                    copy.start()

        @pl.when(at_edge)
        def _():
            for p in range(k * CHUNK // PIECE, (k + 1) * CHUNK // PIECE):
                edge_copy(p).start()

        @pl.when(jnp.logical_not(at_edge))
        def _():
            beside_copies[k].start()

        twin_copies[k].start()

    for k in range(CHUNKS):
        rows = rows_of(k)
        wide = own[rows, :F].astype(f32)
        left[rows, :] = (-2.0 * wide).astype(bf16)
        norm_col[rows, :] = jnp.broadcast_to(jnp.sum(wide * wide, axis=1, keepdims=True), (CHUNK, LANES))
    ids_load.wait()
    own_meta[0:1, :] = norm_col[...].T[0:1, :]
    own_meta[1:2, :] = ids_ref[...].reshape(1, ROWS).astype(f32)

    @pl.when(sends)
    def _():
        far_meta_copy.start()

    for copy in near_meta_copies:
        copy.start()

    def add_block(block, meta):
        tile = matern(left[...], block[:, :F], norm_col[:, 0:1], meta[0:1, :])
        acc[...] += dot(tile, block[:, F:])
        return dot(one_hot(meta[1:2, :]), block[:, F:])

    noise_load.wait()
    acc[...] = noise_ref[...].reshape(1, R) * direction[...]
    dir_t[...] = direction[...].T.astype(bf16)
    spread[...] = one_hot(own_meta[1:2, :]).astype(f32).T.astype(bf16)
    own_totals = add_block(own, own_meta)
    totals[...] = own_totals
    own_halves_t = split_halves(own_totals).astype(f32).T.astype(bf16)

    @pl.when(jnp.logical_not(at_edge))
    def _():
        relay_in.wait_recv()
        relay_copy.start()

    near_meta_copies[0].wait_recv()
    near_whole[0].wait_recv()
    totals[...] += add_block(near.at[0], near_meta.at[0])

    def far_tile(k):
        far_copies[k].wait_recv()
        first_row, size = PARTS[k]
        rows = pl.ds(first_row, size)
        tile = matern(left[...], far[rows, :F], norm_col[:, 0:1], far_meta[0:1, rows])
        spots = one_hot(far_meta[1:2, rows])
        back = dot(dir_t[...], tile) + site_weight * dot(own_halves_t, spots)
        for strip in range(size // LANES):
            ret_out[first_row // LANES + strip] = back[:, strip * LANES:(strip + 1) * LANES].astype(bf16)
        ret_copies[k].start()
        return dot(tile, far[rows, F:]), dot(spots, far[rows, F:])

    def far_part(k):
        products, part_totals = far_tile(k)
        acc[...] += products
        totals[...] += part_totals

    def add_sites():
        acc[...] += site_weight * dot(spread[...], split_halves(totals[...]))

    def add_sums(rows, applied):
        acc[rows, :] = applied
        held, step_rows = residual[rows, :], direction[rows, :]
        sums_ref[1:2, :] += jnp.sum(step_rows * applied, axis=0, keepdims=True)
        sums_ref[2:3, :] += jnp.sum(held * applied, axis=0, keepdims=True)
        sums_ref[3:4, :] += jnp.sum(applied * applied, axis=0, keepdims=True)

    @pl.when(receives)
    def _():
        far_meta_copy.wait_recv()
        far_part(0)
        far_part(1)
        far_part(2)

    near_meta_copies[1].wait_recv()
    near_whole[1].wait_recv()
    totals[...] += add_block(near.at[1], near_meta.at[1])

    res_load.wait()
    sums_ref[...] = jnp.zeros_like(sums_ref)
    sums_ref[0:1, :] = jnp.sum(residual[...] * residual[...], axis=0, keepdims=True)

    @pl.when(receives)
    def _():
        for k in range(3, len(PARTS) - 1):
            far_part(k)
        add_sites()
        products, part_totals = far_tile(len(PARTS) - 1)
        applied = acc[...] + products + site_weight * dot(spread[...], split_halves(part_totals))
        add_sums(pl.ds(0, ROWS), applied)

    @pl.when(sends)
    def _():
        add_sites()
        for k, (first_row, size) in enumerate(PARTS):
            ret_copies[k].wait_recv()
            for strip in range(first_row // LANES, (first_row + size) // LANES):
                rows = pl.ds(strip * LANES, LANES)
                add_sums(rows, acc[rows, :] + ret_in[strip].astype(f32).T)

    def gather_sum(stage, slots, slot, others):
        slots[slot] = sums_ref[...]
        for other in others:
            send(slots.at[slot], slots.at[slot], sum_send.at[stage], sum_recv.at[stage], other).start()
        rest = slots.at[pl.ds(0, len(others))]
        every = send(rest, rest, sum_send.at[stage], sum_recv.at[stage], others[0])
        every.wait_recv()
        sums_ref[...] = jnp.sum(slots[...], axis=0)
        return every

    stages = [gather_sum(0, first, column_place, column), gather_sum(1, second, spot, layer)]
    old_norms, curvature = sums_ref[0:1, :], sums_ref[1:2, :]
    step_size = old_norms / curvature
    new_norms = old_norms - 2.0 * step_size * sums_ref[2:3, :] + step_size * step_size * sums_ref[3:4, :]
    new_norms = jnp.maximum(new_norms, 0.0)
    coef_ref[0:1, :] = step_size
    coef_ref[1:2, :] = new_norms / old_norms
    coef_ref[2:3, :] = new_norms
    coef_ref[3:4, :] = old_norms
    for stage in stages:
        stage.wait_send()

    @pl.when(sends)
    def _():
        far_meta_copy.wait_send()
        for copy in far_copies:
            copy.wait_send()

    @pl.when(receives)
    def _():
        for copy in ret_copies:
            copy.wait_send()

    @pl.when(jnp.logical_not(at_edge))
    def _():
        relay_copy.wait_send()

    for copy in near_meta_copies + near_whole:
        copy.wait_send()


def update(
    sol_ref, res_ref, dir_ref, applied_ref, coef_ref,
    new_sol_hbm, new_res_hbm, new_dir_hbm, norms_hbm,
    made, norms, out_sem,
):
    stores = []

    def store(src, dst, sem):
        stores.append(pltpu.make_async_copy(src, dst, sem))
        stores[-1].start()

    step_size, ratio = coef_ref[0:1, :], coef_ref[1:2, :]
    norms[...] = coef_ref[2:3, :].reshape(R)
    store(norms, norms_hbm, out_sem.at[3 * CHUNKS])
    for k in range(CHUNKS):
        rows = pl.ds(k * CHUNK, CHUNK)
        step_rows = dir_ref[rows, :]
        moved = res_ref[rows, :] - step_size * applied_ref[rows, :]
        made[0, rows, :] = moved
        made[1, rows, :] = sol_ref[rows, :] + step_size * step_rows
        made[2, rows, :] = moved + ratio * step_rows
        for n, out in enumerate((new_res_hbm, new_sol_hbm, new_dir_hbm)):
            store(made.at[n, rows], out.at[rows], out_sem.at[3 * k + n])
    for copy in stores:
        copy.wait()


def body(embeddings, site_ids, inv_scale, noise, solution, residual, direction):
    hbm = pl.BlockSpec(memory_space=pltpu.HBM)
    vmem = pl.BlockSpec(memory_space=pltpu.VMEM)
    dma = pltpu.SemaphoreType.DMA
    applied, held_direction, held_residual, coefs = pl.pallas_call(
        kernel,
        out_shape=(
            pltpu.VMEM((ROWS, R), f32),
            pltpu.VMEM((ROWS, R), f32),
            pltpu.VMEM((ROWS, R), f32),
            pltpu.VMEM((4, R), f32),
        ),
        in_specs=[hbm] * 6,
        out_specs=[vmem] * 4,
        scratch_shapes=[
            pltpu.VMEM((ROWS, F), bf16),
            pltpu.VMEM((ROWS,), jnp.int32),
            pltpu.VMEM((F,), f32),
            pltpu.VMEM((R,), f32),
            pltpu.VMEM((ROWS, F + R), bf16),
            pltpu.VMEM((ROWS, F), bf16),
            pltpu.VMEM((ROWS, 128), f32),
            pltpu.VMEM((R, ROWS), bf16),
            pltpu.VMEM((2, ROWS), f32),
            pltpu.VMEM((2, ROWS, F + R), bf16),
            pltpu.VMEM((2, 2, ROWS), f32),
            pltpu.VMEM((PIECE, F + R), bf16),
            pltpu.VMEM((ROWS, F + R), bf16),
            pltpu.VMEM((2, ROWS), f32),
            pltpu.VMEM((ROWS // LANES, R, LANES), bf16),
            pltpu.VMEM((ROWS // LANES, R, LANES), bf16),
            pltpu.VMEM((2 * sites, R), f32),
            pltpu.VMEM((ROWS, 2 * sites), bf16),
            pltpu.VMEM((4, R), f32),
            pltpu.VMEM((ZS * CS, 4, R), f32),
            pltpu.VMEM((SPOTS, 4, R), f32),
            dma((4 + 2 * CHUNKS,)),
            dma((2,)),
            dma((2,)),
            dma((2,)),
            dma((2,)),
            dma,
            dma,
            dma((len(PARTS),)),
            dma((len(PARTS),)),
            dma,
            dma,
            dma((len(PARTS),)),
            dma((len(PARTS),)),
            dma((2,)),
            dma((2,)),
        ],
        compiler_params=pltpu.CompilerParams(
            collective_id=0, has_side_effects=True, vmem_limit_bytes=56 * 1024 * 1024
        ),
        name="cg_products",
    )(embeddings, direction, residual, site_ids, inv_scale, noise)
    block = jax.ShapeDtypeStruct((ROWS, R), f32)
    new_solution, new_residual, new_direction, new_norms = pl.pallas_call(
        update,
        out_shape=(block, block, block, jax.ShapeDtypeStruct((R,), f32)),
        in_specs=[vmem] * 5,
        out_specs=[hbm] * 4,
        scratch_shapes=[
            pltpu.VMEM((3, ROWS, R), f32),
            pltpu.VMEM((R,), f32),
            dma((3 * CHUNKS + 1,)),
        ],
        compiler_params=pltpu.CompilerParams(vmem_limit_bytes=8 * 1024 * 1024),
        name="cg_update",
    )(solution, held_residual, held_direction, applied, coefs)
    return (new_solution, new_residual, new_direction, new_norms)


def solution(mesh):
    placed = (P("pts", None), P("pts"), P(), P(), P("pts", None), P("pts", None), P("pts", None))
    return jax.shard_map(
        body,
        mesh=mesh,
        in_specs=placed,
        out_specs=(P("pts", None), P("pts", None), P("pts", None), P()),
        check_vma=False,
    )
```

```python
import functools
import math

import jax
import jax.numpy as jnp
from jax import lax
from jax.experimental import pallas as pl
from jax.experimental.pallas import tpu as pltpu
from jax.sharding import PartitionSpec as P

root_three = math.sqrt(3.0)
site_weight = 0.5
sites = 64

MESH = pl.DeviceIdType.MESH
ZS, YS, XS, CS = 8, 4, 4, 2
PLANE = YS * XS * CS
PTS = ZS * PLANE
ROWS = 1024
F = 384
R = 128
CHUNK = 256
CHUNKS = ROWS // CHUNK
LANES = 128
SPOTS = YS * XS
PIECE = ROWS // SPOTS
PARTS = ((0, 384), (384, 384), (768, 256))
f32 = jnp.float32
bf16 = jnp.bfloat16


def dot(a, b):
    return jnp.dot(a, b, preferred_element_type=f32)


def matern(left, right, left_norms, right_norms):
    cross = lax.dot_general(left, right, (((1,), (1,)), ((), ())), preferred_element_type=f32)
    squared = jnp.maximum(cross + left_norms + right_norms, 1e-30)
    distance = squared * lax.rsqrt(squared)
    decay = jnp.exp2(distance * (-root_three * math.log2(math.e)))
    return ((1.0 + root_three * distance) * decay).astype(bf16)


def one_hot(ids):
    rows = lax.broadcasted_iota(jnp.int32, (2 * sites, ids.shape[1]), 0) % sites
    return (rows.astype(f32) == ids).astype(bf16)


def split_halves(totals):
    high = totals.astype(bf16)
    low = (totals - high.astype(f32)).astype(bf16)
    rows = lax.broadcasted_iota(jnp.int32, totals.shape, 0)
    return jnp.where(rows < sites, high, low)


def kernel(
    emb_hbm, dir_hbm, res_hbm, ids_hbm, scale_hbm, noise_hbm,
    acc, direction, residual, coef_ref,
    emb, ids_ref, scale_ref, noise_ref, own, left, norm_col, dir_t, own_meta,
    near, near_meta, relay, far, far_meta, ret_out, ret_in, totals, spread, sums_ref, first, second,
    load_sem, near_send, near_recv, near_meta_send, near_meta_recv,
    relay_send, relay_recv, far_send, far_recv, far_meta_send, far_meta_recv,
    ret_send, ret_recv, sum_send, sum_recv,
):
    me = lax.axis_index("pts")
    core = me % CS
    plane = me // PLANE
    spot = (me // CS) % SPOTS
    place = spot + core * (SPOTS - 1 - 2 * spot)
    at_edge = place == 0

    twin = me + 1 - 2 * core
    step = 2 * core - 1
    beside = (me + step + PTS) % PTS
    opposite = (me + PTS // 2) % PTS
    sends = (me // (PTS // 2) + me) % 2 == 0
    receives = jnp.logical_not(sends)
    next_plane = ((plane + step + ZS) % ZS) * PLANE

    def at_place(base, p, c):
        return base + (p + c * (SPOTS - 1 - 2 * p)) * CS + c

    relays = [at_place(plane * PLANE, p, core) for p in range(SPOTS)]
    next_relays = [at_place(next_plane, p, 1 - core) for p in range(SPOTS)]
    own_edge, next_edge = relays[0], next_relays[0]

    column_place = plane * CS + core
    row, col = spot // XS, spot % XS

    def turn(distance, size):
        return min(distance, size - distance)

    column = [
        ((plane + dz) % ZS) * PLANE + spot * CS + (core + dc) % CS
        for dz in sorted(range(ZS), key=lambda d: -turn(d, ZS)) for dc in range(CS) if dz or dc
    ]
    layer = [
        plane * PLANE + ((row + dy) % YS * XS + (col + dx) % XS) * CS + core
        for dy, dx in sorted(
            ((dy, dx) for dy in range(YS) for dx in range(XS) if dy or dx),
            key=lambda d: -turn(d[0], YS) - turn(d[1], XS),
        )
    ]

    def load(k, src, dst):
        copy = pltpu.make_async_copy(src, dst, load_sem.at[k])
        copy.start()
        return copy

    scale_load = load(0, scale_hbm, scale_ref)
    block_loads = []
    for k in range(CHUNKS):
        rows = pl.ds(k * CHUNK, CHUNK)
        block_loads.append(
            (
                load(4 + 2 * k, emb_hbm.at[rows], emb.at[rows]),
                load(5 + 2 * k, dir_hbm.at[rows], direction.at[rows]),
            )
        )
    ids_load = load(1, ids_hbm, ids_ref)
    noise_load = load(2, noise_hbm, noise_ref)
    res_load = load(3, res_hbm, residual)

    barrier = pltpu.get_barrier_semaphore()
    partners = [other for pair in zip(column, layer) for other in pair] + [beside]
    for other in partners:
        pl.semaphore_signal(barrier, inc=1, device_id=(other,), device_id_type=MESH)

    @pl.when(at_edge)
    def _():
        for other in next_relays[1:]:
            pl.semaphore_signal(barrier, inc=1, device_id=(other,), device_id_type=MESH)

    def send(src, dst, send_sem, recv_sem, other):
        return pltpu.make_async_remote_copy(
            src_ref=src, dst_ref=dst, send_sem=send_sem, recv_sem=recv_sem,
            device_id=(other,), device_id_type=MESH,
        )

    def rows_of(k):
        return pl.ds(k * CHUNK, CHUNK)

    far_copies = [
        send(
            own.at[pl.ds(first_row, size)], far.at[pl.ds(first_row, size)],
            far_send.at[k], far_recv.at[k], opposite,
        )
        for k, (first_row, size) in enumerate(PARTS)
    ]
    twin_copies = [
        send(own.at[rows_of(k)], near.at[0, rows_of(k)], near_send.at[0], near_recv.at[0], twin)
        for k in range(CHUNKS)
    ]
    beside_copies = [
        send(own.at[rows_of(k)], near.at[1, rows_of(k)], near_send.at[1], near_recv.at[1], beside)
        for k in range(CHUNKS)
    ]
    near_whole = [
        send(own, near.at[n], near_send.at[n], near_recv.at[n], other)
        for n, other in enumerate((twin, beside))
    ]

    def piece_of(p):
        return pl.ds(p * PIECE, PIECE)

    def edge_copy(p):
        if p == 0:
            return send(own.at[piece_of(0)], near.at[1, piece_of(0)], near_send.at[1], near_recv.at[1], next_edge)
        return send(own.at[piece_of(p)], relay, near_send.at[1], relay_recv, relays[p])

    held_rows = pl.ds(pl.multiple_of(place * PIECE, PIECE), PIECE)
    relay_copy = send(relay, near.at[1, held_rows], relay_send, near_recv.at[1], next_edge)
    relay_in = send(relay, relay, relay_send, relay_recv, own_edge)
    far_meta_copy = send(own_meta, far_meta, far_meta_send, far_meta_recv, opposite)
    near_meta_copies = [
        send(own_meta, near_meta.at[n], near_meta_send.at[n], near_meta_recv.at[n], other)
        for n, other in enumerate((twin, beside))
    ]
    def strips_of(first_row, size):
        return pl.ds(first_row // LANES, size // LANES)

    ret_copies = [
        send(
            ret_out.at[strips_of(*part)], ret_in.at[strips_of(*part)],
            ret_send.at[k], ret_recv.at[k], opposite,
        )
        for k, part in enumerate(PARTS)
    ]

    scale_load.wait()
    for k in range(CHUNKS):
        rows = rows_of(k)
        for copy in block_loads[k]:
            copy.wait()
        own[rows, :F] = (emb[rows, :].astype(f32) * scale_ref[...].reshape(1, F)).astype(bf16)
        own[rows, F:] = direction[rows, :].astype(bf16)
        if k == 0:
            pl.semaphore_wait(barrier, len(partners) + jnp.where(at_edge, 0, 1))

        @pl.when(sends)
        def _():
            for part, copy in zip(PARTS, far_copies):
                if (part[0] + part[1] - 1) // CHUNK == k:
                    copy.start()

        @pl.when(at_edge)
        def _():
            for p in range(k * CHUNK // PIECE, (k + 1) * CHUNK // PIECE):
                edge_copy(p).start()

        @pl.when(jnp.logical_not(at_edge))
        def _():
            beside_copies[k].start()

        twin_copies[k].start()

    for k in range(CHUNKS):
        rows = rows_of(k)
        wide = own[rows, :F].astype(f32)
        left[rows, :] = (-2.0 * wide).astype(bf16)
        norm_col[rows, :] = jnp.broadcast_to(jnp.sum(wide * wide, axis=1, keepdims=True), (CHUNK, LANES))
    ids_load.wait()
    own_meta[0:1, :] = norm_col[...].T[0:1, :]
    own_meta[1:2, :] = ids_ref[...].reshape(1, ROWS).astype(f32)

    @pl.when(sends)
    def _():
        far_meta_copy.start()

    for copy in near_meta_copies:
        copy.start()

    def add_block(block, meta):
        tile = matern(left[...], block[:, :F], norm_col[:, 0:1], meta[0:1, :])
        acc[...] += dot(tile, block[:, F:])
        return dot(one_hot(meta[1:2, :]), block[:, F:])

    noise_load.wait()
    acc[...] = noise_ref[...].reshape(1, R) * direction[...]
    dir_t[...] = direction[...].T.astype(bf16)
    spread[...] = one_hot(own_meta[1:2, :]).astype(f32).T.astype(bf16)
    own_totals = add_block(own, own_meta)
    totals[...] = own_totals
    own_halves_t = split_halves(own_totals).astype(f32).T.astype(bf16)

    @pl.when(jnp.logical_not(at_edge))
    def _():
        relay_in.wait_recv()
        relay_copy.start()

    near_meta_copies[0].wait_recv()
    near_whole[0].wait_recv()
    totals[...] += add_block(near.at[0], near_meta.at[0])

    def far_tile(k):
        far_copies[k].wait_recv()
        first_row, size = PARTS[k]
        rows = pl.ds(first_row, size)
        tile = matern(left[...], far[rows, :F], norm_col[:, 0:1], far_meta[0:1, rows])
        spots = one_hot(far_meta[1:2, rows])
        back = dot(dir_t[...], tile) + site_weight * dot(own_halves_t, spots)
        for strip in range(size // LANES):
            ret_out[first_row // LANES + strip] = back[:, strip * LANES:(strip + 1) * LANES].astype(bf16)
        ret_copies[k].start()
        return dot(tile, far[rows, F:]), dot(spots, far[rows, F:])

    def far_part(k):
        products, part_totals = far_tile(k)
        acc[...] += products
        totals[...] += part_totals

    def add_sites():
        acc[...] += site_weight * dot(spread[...], split_halves(totals[...]))

    def add_sums(rows, applied):
        acc[rows, :] = applied
        held, step_rows = residual[rows, :], direction[rows, :]
        sums_ref[1:2, :] += jnp.sum(step_rows * applied, axis=0, keepdims=True)
        sums_ref[2:3, :] += jnp.sum(held * applied, axis=0, keepdims=True)
        sums_ref[3:4, :] += jnp.sum(applied * applied, axis=0, keepdims=True)

    @pl.when(receives)
    def _():
        far_meta_copy.wait_recv()
        far_part(0)
        far_part(1)

    near_meta_copies[1].wait_recv()
    near_whole[1].wait_recv()
    totals[...] += add_block(near.at[1], near_meta.at[1])

    res_load.wait()
    sums_ref[...] = jnp.zeros_like(sums_ref)
    sums_ref[0:1, :] = jnp.sum(residual[...] * residual[...], axis=0, keepdims=True)

    @pl.when(receives)
    def _():
        for k in range(2, len(PARTS) - 1):
            far_part(k)
        add_sites()
        products, part_totals = far_tile(len(PARTS) - 1)
        applied = acc[...] + products + site_weight * dot(spread[...], split_halves(part_totals))
        add_sums(pl.ds(0, ROWS), applied)

    @pl.when(sends)
    def _():
        add_sites()
        for k, (first_row, size) in enumerate(PARTS):
            ret_copies[k].wait_recv()
            for strip in range(first_row // LANES, (first_row + size) // LANES):
                rows = pl.ds(strip * LANES, LANES)
                add_sums(rows, acc[rows, :] + ret_in[strip].astype(f32).T)

    def gather_sum(stage, slots, slot, others):
        slots[slot] = sums_ref[...]
        for other in others:
            send(slots.at[slot], slots.at[slot], sum_send.at[stage], sum_recv.at[stage], other).start()
        rest = slots.at[pl.ds(0, len(others))]
        every = send(rest, rest, sum_send.at[stage], sum_recv.at[stage], others[0])
        every.wait_recv()
        sums_ref[...] = jnp.sum(slots[...], axis=0)
        return every

    stages = [gather_sum(0, first, column_place, column), gather_sum(1, second, spot, layer)]
    old_norms, curvature = sums_ref[0:1, :], sums_ref[1:2, :]
    step_size = old_norms / curvature
    new_norms = old_norms - 2.0 * step_size * sums_ref[2:3, :] + step_size * step_size * sums_ref[3:4, :]
    new_norms = jnp.maximum(new_norms, 0.0)
    coef_ref[0:1, :] = step_size
    coef_ref[1:2, :] = new_norms / old_norms
    coef_ref[2:3, :] = new_norms
    coef_ref[3:4, :] = old_norms
    for stage in stages:
        stage.wait_send()

    @pl.when(sends)
    def _():
        far_meta_copy.wait_send()
        for copy in far_copies:
            copy.wait_send()

    @pl.when(receives)
    def _():
        for copy in ret_copies:
            copy.wait_send()

    @pl.when(jnp.logical_not(at_edge))
    def _():
        relay_copy.wait_send()

    for copy in near_meta_copies + near_whole:
        copy.wait_send()


def update(
    sol_ref, res_ref, dir_ref, applied_ref, coef_ref,
    new_sol_hbm, new_res_hbm, new_dir_hbm, norms_hbm,
    made, norms, out_sem,
):
    stores = []

    def store(src, dst, sem):
        stores.append(pltpu.make_async_copy(src, dst, sem))
        stores[-1].start()

    step_size, ratio = coef_ref[0:1, :], coef_ref[1:2, :]
    norms[...] = coef_ref[2:3, :].reshape(R)
    store(norms, norms_hbm, out_sem.at[3 * CHUNKS])
    for k in range(CHUNKS):
        rows = pl.ds(k * CHUNK, CHUNK)
        step_rows = dir_ref[rows, :]
        moved = res_ref[rows, :] - step_size * applied_ref[rows, :]
        made[0, rows, :] = moved
        made[1, rows, :] = sol_ref[rows, :] + step_size * step_rows
        made[2, rows, :] = moved + ratio * step_rows
        for n, out in enumerate((new_res_hbm, new_sol_hbm, new_dir_hbm)):
            store(made.at[n, rows], out.at[rows], out_sem.at[3 * k + n])
    for copy in stores:
        copy.wait()


def body(embeddings, site_ids, inv_scale, noise, solution, residual, direction):
    hbm = pl.BlockSpec(memory_space=pltpu.HBM)
    vmem = pl.BlockSpec(memory_space=pltpu.VMEM)
    dma = pltpu.SemaphoreType.DMA
    applied, held_direction, held_residual, coefs = pl.pallas_call(
        kernel,
        out_shape=(
            pltpu.VMEM((ROWS, R), f32),
            pltpu.VMEM((ROWS, R), f32),
            pltpu.VMEM((ROWS, R), f32),
            pltpu.VMEM((4, R), f32),
        ),
        in_specs=[hbm] * 6,
        out_specs=[vmem] * 4,
        scratch_shapes=[
            pltpu.VMEM((ROWS, F), bf16),
            pltpu.VMEM((ROWS,), jnp.int32),
            pltpu.VMEM((F,), f32),
            pltpu.VMEM((R,), f32),
            pltpu.VMEM((ROWS, F + R), bf16),
            pltpu.VMEM((ROWS, F), bf16),
            pltpu.VMEM((ROWS, 128), f32),
            pltpu.VMEM((R, ROWS), bf16),
            pltpu.VMEM((2, ROWS), f32),
            pltpu.VMEM((2, ROWS, F + R), bf16),
            pltpu.VMEM((2, 2, ROWS), f32),
            pltpu.VMEM((PIECE, F + R), bf16),
            pltpu.VMEM((ROWS, F + R), bf16),
            pltpu.VMEM((2, ROWS), f32),
            pltpu.VMEM((ROWS // LANES, R, LANES), bf16),
            pltpu.VMEM((ROWS // LANES, R, LANES), bf16),
            pltpu.VMEM((2 * sites, R), f32),
            pltpu.VMEM((ROWS, 2 * sites), bf16),
            pltpu.VMEM((4, R), f32),
            pltpu.VMEM((ZS * CS, 4, R), f32),
            pltpu.VMEM((SPOTS, 4, R), f32),
            dma((4 + 2 * CHUNKS,)),
            dma((2,)),
            dma((2,)),
            dma((2,)),
            dma((2,)),
            dma,
            dma,
            dma((len(PARTS),)),
            dma((len(PARTS),)),
            dma,
            dma,
            dma((len(PARTS),)),
            dma((len(PARTS),)),
            dma((2,)),
            dma((2,)),
        ],
        compiler_params=pltpu.CompilerParams(
            collective_id=0, has_side_effects=True, vmem_limit_bytes=56 * 1024 * 1024
        ),
        name="cg_products",
    )(embeddings, direction, residual, site_ids, inv_scale, noise)
    block = jax.ShapeDtypeStruct((ROWS, R), f32)
    new_solution, new_residual, new_direction, new_norms = pl.pallas_call(
        update,
        out_shape=(block, block, block, jax.ShapeDtypeStruct((R,), f32)),
        in_specs=[vmem] * 5,
        out_specs=[hbm] * 4,
        scratch_shapes=[
            pltpu.VMEM((3, ROWS, R), f32),
            pltpu.VMEM((R,), f32),
            dma((3 * CHUNKS + 1,)),
        ],
        compiler_params=pltpu.CompilerParams(vmem_limit_bytes=8 * 1024 * 1024),
        name="cg_update",
    )(solution, held_residual, held_direction, applied, coefs)
    return (new_solution, new_residual, new_direction, new_norms)


def solution(mesh):
    placed = (P("pts", None), P("pts"), P(), P(), P("pts", None), P("pts", None), P("pts", None))
    return jax.shard_map(
        body,
        mesh=mesh,
        in_specs=placed,
        out_specs=(P("pts", None), P("pts", None), P("pts", None), P()),
        check_vma=False,
    )
```

```python
import functools
import math

import jax
import jax.numpy as jnp
from jax import lax
from jax.experimental import pallas as pl
from jax.experimental.pallas import tpu as pltpu
from jax.sharding import PartitionSpec as P

root_three = math.sqrt(3.0)
site_weight = 0.5
sites = 64

MESH = pl.DeviceIdType.MESH
ZS, YS, XS, CS = 8, 4, 4, 2
PLANE = YS * XS * CS
PTS = ZS * PLANE
ROWS = 1024
F = 384
R = 128
CHUNK = 256
CHUNKS = ROWS // CHUNK
LANES = 128
SPOTS = YS * XS
PIECE = ROWS // SPOTS
PARTS = ((0, 256), (256, 256), (512, 256), (768, 128), (896, 128))
f32 = jnp.float32
bf16 = jnp.bfloat16


def dot(a, b):
    return jnp.dot(a, b, preferred_element_type=f32)


def matern(left, right, left_norms, right_norms):
    cross = lax.dot_general(left, right, (((1,), (1,)), ((), ())), preferred_element_type=f32)
    squared = jnp.maximum(cross + left_norms + right_norms, 1e-30)
    distance = squared * lax.rsqrt(squared)
    decay = jnp.exp2(distance * (-root_three * math.log2(math.e)))
    return ((1.0 + root_three * distance) * decay).astype(bf16)


def one_hot(ids):
    rows = lax.broadcasted_iota(jnp.int32, (2 * sites, ids.shape[1]), 0) % sites
    return (rows.astype(f32) == ids).astype(bf16)


def split_halves(totals):
    high = totals.astype(bf16)
    low = (totals - high.astype(f32)).astype(bf16)
    rows = lax.broadcasted_iota(jnp.int32, totals.shape, 0)
    return jnp.where(rows < sites, high, low)


def kernel(
    emb_hbm, dir_hbm, res_hbm, ids_hbm, scale_hbm, noise_hbm,
    acc, direction, residual, coef_ref,
    emb, ids_ref, scale_ref, noise_ref, own, left, norm_col, dir_t, own_meta,
    near, near_meta, relay, far, far_meta, ret_out, ret_in, totals, spread, sums_ref, first, second,
    load_sem, near_send, near_recv, near_meta_send, near_meta_recv,
    relay_send, relay_recv, far_send, far_recv, far_meta_send, far_meta_recv,
    ret_send, ret_recv, sum_send, sum_recv,
):
    me = lax.axis_index("pts")
    core = me % CS
    plane = me // PLANE
    spot = (me // CS) % SPOTS
    place = spot + core * (SPOTS - 1 - 2 * spot)
    at_edge = place == 0

    twin = me + 1 - 2 * core
    step = 2 * core - 1
    beside = (me + step + PTS) % PTS
    opposite = (me + PTS // 2) % PTS
    sends = (me // (PTS // 2) + me) % 2 == 0
    receives = jnp.logical_not(sends)
    next_plane = ((plane + step + ZS) % ZS) * PLANE

    def at_place(base, p, c):
        return base + (p + c * (SPOTS - 1 - 2 * p)) * CS + c

    relays = [at_place(plane * PLANE, p, core) for p in range(SPOTS)]
    next_relays = [at_place(next_plane, p, 1 - core) for p in range(SPOTS)]
    own_edge, next_edge = relays[0], next_relays[0]

    column_place = plane * CS + core
    row, col = spot // XS, spot % XS

    def turn(distance, size):
        return min(distance, size - distance)

    column = [
        ((plane + dz) % ZS) * PLANE + spot * CS + (core + dc) % CS
        for dz in sorted(range(ZS), key=lambda d: -turn(d, ZS)) for dc in range(CS) if dz or dc
    ]
    layer = [
        plane * PLANE + ((row + dy) % YS * XS + (col + dx) % XS) * CS + core
        for dy, dx in sorted(
            ((dy, dx) for dy in range(YS) for dx in range(XS) if dy or dx),
            key=lambda d: -turn(d[0], YS) - turn(d[1], XS),
        )
    ]

    def load(k, src, dst):
        copy = pltpu.make_async_copy(src, dst, load_sem.at[k])
        copy.start()
        return copy

    scale_load = load(0, scale_hbm, scale_ref)
    block_loads = []
    for k in range(CHUNKS):
        rows = pl.ds(k * CHUNK, CHUNK)
        block_loads.append(
            (
                load(4 + 2 * k, emb_hbm.at[rows], emb.at[rows]),
                load(5 + 2 * k, dir_hbm.at[rows], direction.at[rows]),
            )
        )
    ids_load = load(1, ids_hbm, ids_ref)
    noise_load = load(2, noise_hbm, noise_ref)
    res_load = load(3, res_hbm, residual)

    barrier = pltpu.get_barrier_semaphore()
    partners = [other for pair in zip(column, layer) for other in pair] + [beside]
    for other in partners:
        pl.semaphore_signal(barrier, inc=1, device_id=(other,), device_id_type=MESH)

    @pl.when(at_edge)
    def _():
        for other in next_relays[1:]:
            pl.semaphore_signal(barrier, inc=1, device_id=(other,), device_id_type=MESH)

    def send(src, dst, send_sem, recv_sem, other):
        return pltpu.make_async_remote_copy(
            src_ref=src, dst_ref=dst, send_sem=send_sem, recv_sem=recv_sem,
            device_id=(other,), device_id_type=MESH,
        )

    def rows_of(k):
        return pl.ds(k * CHUNK, CHUNK)

    far_copies = [
        send(
            own.at[pl.ds(first_row, size)], far.at[pl.ds(first_row, size)],
            far_send.at[k], far_recv.at[k], opposite,
        )
        for k, (first_row, size) in enumerate(PARTS)
    ]
    twin_copies = [
        send(own.at[rows_of(k)], near.at[0, rows_of(k)], near_send.at[0], near_recv.at[0], twin)
        for k in range(CHUNKS)
    ]
    beside_copies = [
        send(own.at[rows_of(k)], near.at[1, rows_of(k)], near_send.at[1], near_recv.at[1], beside)
        for k in range(CHUNKS)
    ]
    near_whole = [
        send(own, near.at[n], near_send.at[n], near_recv.at[n], other)
        for n, other in enumerate((twin, beside))
    ]

    def piece_of(p):
        return pl.ds(p * PIECE, PIECE)

    def edge_copy(p):
        if p == 0:
            return send(own.at[piece_of(0)], near.at[1, piece_of(0)], near_send.at[1], near_recv.at[1], next_edge)
        return send(own.at[piece_of(p)], relay, near_send.at[1], relay_recv, relays[p])

    held_rows = pl.ds(pl.multiple_of(place * PIECE, PIECE), PIECE)
    relay_copy = send(relay, near.at[1, held_rows], relay_send, near_recv.at[1], next_edge)
    relay_in = send(relay, relay, relay_send, relay_recv, own_edge)
    far_meta_copy = send(own_meta, far_meta, far_meta_send, far_meta_recv, opposite)
    near_meta_copies = [
        send(own_meta, near_meta.at[n], near_meta_send.at[n], near_meta_recv.at[n], other)
        for n, other in enumerate((twin, beside))
    ]
    def strips_of(first_row, size):
        return pl.ds(first_row // LANES, size // LANES)

    ret_copies = [
        send(
            ret_out.at[strips_of(*part)], ret_in.at[strips_of(*part)],
            ret_send.at[k], ret_recv.at[k], opposite,
        )
        for k, part in enumerate(PARTS)
    ]

    scale_load.wait()
    for k in range(CHUNKS):
        rows = rows_of(k)
        for copy in block_loads[k]:
            copy.wait()
        own[rows, :F] = (emb[rows, :].astype(f32) * scale_ref[...].reshape(1, F)).astype(bf16)
        own[rows, F:] = direction[rows, :].astype(bf16)
        if k == 0:
            pl.semaphore_wait(barrier, len(partners) + jnp.where(at_edge, 0, 1))

        @pl.when(sends)
        def _():
            for part, copy in zip(PARTS, far_copies):
                if (part[0] + part[1] - 1) // CHUNK == k:
                    copy.start()

        @pl.when(at_edge)
        def _():
            for p in range(k * CHUNK // PIECE, (k + 1) * CHUNK // PIECE):
                edge_copy(p).start()

        @pl.when(jnp.logical_not(at_edge))
        def _():
            beside_copies[k].start()

        twin_copies[k].start()

    for k in range(CHUNKS):
        rows = rows_of(k)
        wide = own[rows, :F].astype(f32)
        left[rows, :] = (-2.0 * wide).astype(bf16)
        norm_col[rows, :] = jnp.broadcast_to(jnp.sum(wide * wide, axis=1, keepdims=True), (CHUNK, LANES))
    ids_load.wait()
    own_meta[0:1, :] = norm_col[...].T[0:1, :]
    own_meta[1:2, :] = ids_ref[...].reshape(1, ROWS).astype(f32)

    @pl.when(sends)
    def _():
        far_meta_copy.start()

    for copy in near_meta_copies:
        copy.start()

    def add_block(block, meta):
        def some_rows(t, carry):
            rows = pl.ds(pl.multiple_of(t * 256, 256), 256)
            tile = matern(left[rows, :], block[:, :F], norm_col[rows, 0:1], meta[0:1, :])
            acc[rows, :] += dot(tile, block[:, F:])
            return carry

        lax.fori_loop(0, ROWS // 256, some_rows, 0)
        return dot(one_hot(meta[1:2, :]), block[:, F:])

    noise_load.wait()
    acc[...] = noise_ref[...].reshape(1, R) * direction[...]
    dir_t[...] = direction[...].T.astype(bf16)
    spread[...] = one_hot(own_meta[1:2, :]).astype(f32).T.astype(bf16)
    own_totals = add_block(own, own_meta)
    totals[...] = own_totals
    own_halves_t = split_halves(own_totals).astype(f32).T.astype(bf16)

    @pl.when(jnp.logical_not(at_edge))
    def _():
        relay_in.wait_recv()
        relay_copy.start()

    near_meta_copies[0].wait_recv()
    near_whole[0].wait_recv()
    totals[...] += add_block(near.at[0], near_meta.at[0])

    def far_part(k):
        first_row, size = PARTS[k]
        rows = pl.ds(first_row, size)
        spots = one_hot(far_meta[1:2, rows])
        back_sites = site_weight * dot(own_halves_t, spots)
        far_copies[k].wait_recv()
        tile = matern(left[...], far[rows, :F], norm_col[:, 0:1], far_meta[0:1, rows])
        back = dot(dir_t[...], tile) + back_sites
        for strip in range(size // LANES):
            ret_out[first_row // LANES + strip] = back[:, strip * LANES:(strip + 1) * LANES].astype(bf16)
        ret_copies[k].start()
        acc[...] += dot(tile, far[rows, F:])
        totals[...] += dot(spots, far[rows, F:])

    def add_sites():
        acc[...] += site_weight * dot(spread[...], split_halves(totals[...]))

    def add_sums(rows, applied):
        acc[rows, :] = applied
        held, step_rows = residual[rows, :], direction[rows, :]
        sums_ref[1:2, :] += jnp.sum(step_rows * applied, axis=0, keepdims=True)
        sums_ref[2:3, :] += jnp.sum(held * applied, axis=0, keepdims=True)
        sums_ref[3:4, :] += jnp.sum(applied * applied, axis=0, keepdims=True)

    @pl.when(receives)
    def _():
        far_meta_copy.wait_recv()
        for k in range(len(PARTS)):
            far_part(k)

    near_meta_copies[1].wait_recv()
    near_whole[1].wait_recv()
    totals[...] += add_block(near.at[1], near_meta.at[1])

    res_load.wait()
    sums_ref[...] = jnp.zeros_like(sums_ref)
    sums_ref[0:1, :] = jnp.sum(residual[...] * residual[...], axis=0, keepdims=True)
    add_sites()

    @pl.when(receives)
    def _():
        add_sums(pl.ds(0, ROWS), acc[...])

    @pl.when(sends)
    def _():
        for k, (first_row, size) in enumerate(PARTS):
            ret_copies[k].wait_recv()
            for strip in range(first_row // LANES, (first_row + size) // LANES):
                rows = pl.ds(strip * LANES, LANES)
                add_sums(rows, acc[rows, :] + ret_in[strip].astype(f32).T)

    def gather_sum(stage, slots, slot, others):
        slots[slot] = sums_ref[...]
        for other in others:
            send(slots.at[slot], slots.at[slot], sum_send.at[stage], sum_recv.at[stage], other).start()
        rest = slots.at[pl.ds(0, len(others))]
        every = send(rest, rest, sum_send.at[stage], sum_recv.at[stage], others[0])
        every.wait_recv()
        sums_ref[...] = jnp.sum(slots[...], axis=0)
        return every

    stages = [gather_sum(0, first, column_place, column), gather_sum(1, second, spot, layer)]
    old_norms, curvature = sums_ref[0:1, :], sums_ref[1:2, :]
    step_size = old_norms / curvature
    new_norms = old_norms - 2.0 * step_size * sums_ref[2:3, :] + step_size * step_size * sums_ref[3:4, :]
    new_norms = jnp.maximum(new_norms, 0.0)
    coef_ref[0:1, :] = step_size
    coef_ref[1:2, :] = new_norms / old_norms
    coef_ref[2:3, :] = new_norms
    coef_ref[3:4, :] = old_norms
    for stage in stages:
        stage.wait_send()

    @pl.when(sends)
    def _():
        far_meta_copy.wait_send()
        for copy in far_copies:
            copy.wait_send()

    @pl.when(receives)
    def _():
        for copy in ret_copies:
            copy.wait_send()

    @pl.when(jnp.logical_not(at_edge))
    def _():
        relay_copy.wait_send()

    for copy in near_meta_copies + near_whole:
        copy.wait_send()


def update(
    sol_ref, res_ref, dir_ref, applied_ref, coef_ref,
    new_sol_hbm, new_res_hbm, new_dir_hbm, norms_hbm,
    made, norms, out_sem,
):
    stores = []

    def store(src, dst, sem):
        stores.append(pltpu.make_async_copy(src, dst, sem))
        stores[-1].start()

    step_size, ratio = coef_ref[0:1, :], coef_ref[1:2, :]
    norms[...] = coef_ref[2:3, :].reshape(R)
    store(norms, norms_hbm, out_sem.at[3 * CHUNKS])
    for k in range(CHUNKS):
        rows = pl.ds(k * CHUNK, CHUNK)
        step_rows = dir_ref[rows, :]
        moved = res_ref[rows, :] - step_size * applied_ref[rows, :]
        made[0, rows, :] = moved
        made[1, rows, :] = sol_ref[rows, :] + step_size * step_rows
        made[2, rows, :] = moved + ratio * step_rows
        for n, out in enumerate((new_res_hbm, new_sol_hbm, new_dir_hbm)):
            store(made.at[n, rows], out.at[rows], out_sem.at[3 * k + n])
    for copy in stores:
        copy.wait()


def body(embeddings, site_ids, inv_scale, noise, solution, residual, direction):
    hbm = pl.BlockSpec(memory_space=pltpu.HBM)
    vmem = pl.BlockSpec(memory_space=pltpu.VMEM)
    dma = pltpu.SemaphoreType.DMA
    applied, held_direction, held_residual, coefs = pl.pallas_call(
        kernel,
        out_shape=(
            pltpu.VMEM((ROWS, R), f32),
            pltpu.VMEM((ROWS, R), f32),
            pltpu.VMEM((ROWS, R), f32),
            pltpu.VMEM((4, R), f32),
        ),
        in_specs=[hbm] * 6,
        out_specs=[vmem] * 4,
        scratch_shapes=[
            pltpu.VMEM((ROWS, F), bf16),
            pltpu.VMEM((ROWS,), jnp.int32),
            pltpu.VMEM((F,), f32),
            pltpu.VMEM((R,), f32),
            pltpu.VMEM((ROWS, F + R), bf16),
            pltpu.VMEM((ROWS, F), bf16),
            pltpu.VMEM((ROWS, 128), f32),
            pltpu.VMEM((R, ROWS), bf16),
            pltpu.VMEM((2, ROWS), f32),
            pltpu.VMEM((2, ROWS, F + R), bf16),
            pltpu.VMEM((2, 2, ROWS), f32),
            pltpu.VMEM((PIECE, F + R), bf16),
            pltpu.VMEM((ROWS, F + R), bf16),
            pltpu.VMEM((2, ROWS), f32),
            pltpu.VMEM((ROWS // LANES, R, LANES), bf16),
            pltpu.VMEM((ROWS // LANES, R, LANES), bf16),
            pltpu.VMEM((2 * sites, R), f32),
            pltpu.VMEM((ROWS, 2 * sites), bf16),
            pltpu.VMEM((4, R), f32),
            pltpu.VMEM((ZS * CS, 4, R), f32),
            pltpu.VMEM((SPOTS, 4, R), f32),
            dma((4 + 2 * CHUNKS,)),
            dma((2,)),
            dma((2,)),
            dma((2,)),
            dma((2,)),
            dma,
            dma,
            dma((len(PARTS),)),
            dma((len(PARTS),)),
            dma,
            dma,
            dma((len(PARTS),)),
            dma((len(PARTS),)),
            dma((2,)),
            dma((2,)),
        ],
        compiler_params=pltpu.CompilerParams(
            collective_id=0, has_side_effects=True, vmem_limit_bytes=56 * 1024 * 1024
        ),
        name="cg_products",
    )(embeddings, direction, residual, site_ids, inv_scale, noise)
    block = jax.ShapeDtypeStruct((ROWS, R), f32)
    new_solution, new_residual, new_direction, new_norms = pl.pallas_call(
        update,
        out_shape=(block, block, block, jax.ShapeDtypeStruct((R,), f32)),
        in_specs=[vmem] * 5,
        out_specs=[hbm] * 4,
        scratch_shapes=[
            pltpu.VMEM((3, ROWS, R), f32),
            pltpu.VMEM((R,), f32),
            dma((3 * CHUNKS + 1,)),
        ],
        compiler_params=pltpu.CompilerParams(vmem_limit_bytes=8 * 1024 * 1024),
        name="cg_update",
    )(solution, held_residual, held_direction, applied, coefs)
    return (new_solution, new_residual, new_direction, new_norms)


def solution(mesh):
    placed = (P("pts", None), P("pts"), P(), P(), P("pts", None), P("pts", None), P("pts", None))
    return jax.shard_map(
        body,
        mesh=mesh,
        in_specs=placed,
        out_specs=(P("pts", None), P("pts", None), P("pts", None), P()),
        check_vma=False,
    )
```
